32 devices in a mesh: dp: 2 (over core), graph: 16 (over z, y, x).
Axes of the slice: x: 2, y: 2, z: 4, core: 2. Of those that a mesh axis runs over, the one named last changes fastest.
Arguments:
- node_latents: bfloat16 [8, 5120, 512], P('dp', 'graph'), may hold values from -6 to 6
- edge_latents: bfloat16 [8, 40960, 512], P('dp', 'graph'), may hold values from -6 to 6
- edge_first: bfloat16 [1536, 512], replicated, may hold values from -0.15625 to 0.15625
- edge_first_bias: float32 [512], replicated, may hold values from -3 to 3
- edge_second: bfloat16 [512, 512], replicated, may hold values from -0.25 to 0.25
- edge_second_bias: float32 [512], replicated, may hold values from -3 to 3
- edge_gain: float32 [512], replicated, may hold values from 0.5 to 1.5
- edge_shift: float32 [512], replicated, may hold values from -2 to 2
- node_first: bfloat16 [1024, 512], replicated, may hold values from -0.1875 to 0.1875
- node_first_bias: float32 [512], replicated, may hold values from -3 to 3
- node_second: bfloat16 [512, 512], replicated, may hold values from -0.25 to 0.25
- node_second_bias: float32 [512], replicated, may hold values from -3 to 3
- node_gain: float32 [512], replicated, may hold values from 0.5 to 1.5
- node_shift: float32 [512], replicated, may hold values from -2 to 2
- node_cot: bfloat16 [8, 5120, 512], P('dp', 'graph'), may hold values from -6 to 6
- edge_cot: bfloat16 [8, 40960, 512], P('dp', 'graph'), may hold values from -6 to 6
- send_index: int32 [16, 16, 12], P('graph'), may hold values from 0 to 317, as said below
- edge_sender: int32 [40960], P('graph'), may hold values from 0 to 511, as said below
- edge_receiver: int32 [40960], P('graph'), may hold values from 0 to 319, as said below
- node_mask: int32 [5120], P('graph'), may hold values from 0 to 1, as said below
Outputs:
- nodes_out: bfloat16 [8, 5120, 512], P('dp', 'graph')
- edges_out: bfloat16 [8, 40960, 512], P('dp', 'graph')
- node_grad: float32 [8, 5120, 512], P('dp', 'graph')
- edge_grad: bfloat16 [8, 40960, 512], P('dp', 'graph')
- edge_first_grad: float32 [1536, 512], replicated
- edge_first_bias_grad: float32 [512], replicated
- edge_second_grad: float32 [512, 512], replicated
- edge_second_bias_grad: float32 [512], replicated
- edge_gain_grad: float32 [512], replicated
- edge_shift_grad: float32 [512], replicated
- node_first_grad: float32 [1024, 512], replicated
- node_first_bias_grad: float32 [512], replicated
- node_second_grad: float32 [512, 512], replicated
- node_second_bias_grad: float32 [512], replicated
- node_gain_grad: float32 [512], replicated
- node_shift_grad: float32 [512], replicated
The draws below stay inside these ranges and needn't reach their ends.
Inputs may be any that keep to these rules, and one draw needn't show every extreme that they name: `send_index`: each entry is a live node (mask 1) of the sending block, the first index. `edge_sender`: below 320: a live node of the edge's own block. Otherwise the received slot as in the reference program. Senders of edges with a padding receiver are arbitrary in range. `edge_receiver`: never decreases within a block's 2560 edges. An edge is live iff its receiver is live; the others come last in their block and point to node 319. Some block has all its edges live. `node_mask`: in each block of 320 nodes the live ones come first, at least half of them; the last 2 are padding.
All inputs are finite; a program needn't handle non-finite values.
Results may differ from the reference program's by a relative error of at most 0.0083.
Values may be sent and summed in bfloat16 or wider, within the bound.
No kernel may reach another device: no remote copies, remote signals or barrier semaphores. Data moves between devices by JAX's collectives and lax.ppermute only.
A program may use at most 320 MiB of HBM per device.

```python
import jax
import jax.numpy as jnp
from jax import lax

D = 512
NODE_DEV = 320
NEAR = 16
CAP = 12
EDGE_DEV = 2560
GRAPH_BLOCKS = 16
SAMPLES = 8
NODES = 5120
EDGES = 40960


def live_counts(key):
    node_key, edge_key, pick_key = jax.random.split(key, 3)
    node_count = jax.random.randint(node_key, (GRAPH_BLOCKS,), NODE_DEV // 2, NODE_DEV - 1)
    edge_count = jax.random.randint(edge_key, (GRAPH_BLOCKS,), EDGE_DEV // 2, EDGE_DEV)
    full_block = jax.random.randint(pick_key, (), 0, GRAPH_BLOCKS)
    edge_count = edge_count.at[full_block].set(EDGE_DEV)
    node_count = node_count.at[full_block].set(NODE_DEV - 2)
    return (node_count, edge_count, full_block)


def draw_node_mask(key, part):
    node_count, edge_count, full_block = live_counts(key)
    positions = jnp.arange(NODE_DEV, dtype=jnp.int32)
    return (positions[None, :] < node_count[:, None]).astype(jnp.int32).reshape(NODES)


def draw_edge_receiver(key, part):
    node_count, edge_count, full_block = live_counts(key)
    key = jax.random.fold_in(key, 12)
    drawn = jax.random.randint(key, (GRAPH_BLOCKS, EDGE_DEV), 0, 1 << 20)
    picked = drawn * node_count[:, None] // (1 << 20)
    positions = jnp.arange(EDGE_DEV, dtype=jnp.int32)[None, :]
    picked = jnp.where(positions < edge_count[:, None], picked, NODE_DEV - 1)
    return jnp.sort(picked, axis=1).reshape(EDGES).astype(jnp.int32)


def draw_edge_sender(key, part):
    node_count, edge_count, full_block = live_counts(key)
    key = jax.random.fold_in(key, 13)
    flag_key, local_key, halo_key = jax.random.split(key, 3)
    remote = jax.random.randint(flag_key, (GRAPH_BLOCKS, EDGE_DEV), 0, 4) == 0
    drawn = jax.random.randint(local_key, (GRAPH_BLOCKS, EDGE_DEV), 0, 1 << 20)
    local_pick = drawn * node_count[:, None] // (1 << 20)
    halo_pick = NODE_DEV + jax.random.randint(halo_key, (GRAPH_BLOCKS, EDGE_DEV), 0, NEAR * CAP)
    chosen = jnp.where(remote, halo_pick, local_pick)
    chosen = chosen.at[0, 0].set(NODE_DEV + NEAR * CAP - 1)
    return chosen.reshape(EDGES).astype(jnp.int32)


def draw_send_index(key, part):
    node_count, edge_count, full_block = live_counts(key)
    key = jax.random.fold_in(key, 14)
    drawn = jax.random.randint(key, (GRAPH_BLOCKS, NEAR, CAP), 0, 1 << 20)
    picked = drawn * node_count[:, None, None] // (1 << 20)
    picked = picked.at[:, :, 0].set(0)
    picked = picked.at[full_block, 0, 0].set(NODE_DEV - 3)
    return picked.astype(jnp.int32)


def level_of(stream_key, shape, shards, smallest, top_value):
    level, own = 1.0, jax.random.fold_in(stream_key, 6)
    for axis_at, blocks in shards:
        steps = jnp.exp(jax.random.uniform(jax.random.fold_in(own, axis_at), (blocks,), jnp.float32, smallest / len(shards), top_value / len(shards)))
        level = level * jnp.repeat(steps, shape[axis_at] // blocks).reshape([-1 if axis == axis_at else 1 for axis in range(len(shape))])
    return level


def noise(rng, shape, deviation, reach, cuts=(), kind=jnp.bfloat16):
    loudness = level_of(rng, shape, cuts, -0.22, 0.18) if cuts else 1.0
    array = jax.random.normal(rng, shape, jnp.float32) * deviation * loudness
    return jnp.minimum(jnp.maximum(array, -reach), reach).astype(kind)


def setup_inputs(seed: int = 0) -> dict:
    seeds = jax.random.split(jax.random.key(seed), 21)
    return {
        "node_latents": noise(seeds[0], (SAMPLES, NODES, D), 1.0, 6.0, ((0, 2), (1, 16))),
        "edge_latents": noise(seeds[1], (SAMPLES, EDGES, D), 1.0, 6.0, ((0, 2), (1, 16))),
        "edge_first": noise(seeds[2], (3 * D, D), (3 * D) ** -0.5, 0.15625),
        "edge_first_bias": noise(seeds[3], (D,), 0.5, 3.0, (), jnp.float32),
        "edge_second": noise(seeds[4], (D, D), D ** -0.5, 0.25),
        "edge_second_bias": noise(seeds[5], (D,), 0.5, 3.0, (), jnp.float32),
        "edge_gain": jnp.clip(1.0 + 0.1 * jax.random.normal(seeds[6], (D,), jnp.float32), 0.5, 1.5),
        "edge_shift": noise(seeds[7], (D,), 0.3, 2.0, (), jnp.float32),
        "node_first": noise(seeds[8], (2 * D, D), (2 * D) ** -0.5, 0.1875),
        "node_first_bias": noise(seeds[9], (D,), 0.5, 3.0, (), jnp.float32),
        "node_second": noise(seeds[10], (D, D), D ** -0.5, 0.25),
        "node_second_bias": noise(seeds[11], (D,), 0.5, 3.0, (), jnp.float32),
        "node_gain": jnp.clip(1.0 + 0.1 * jax.random.normal(seeds[12], (D,), jnp.float32), 0.5, 1.5),
        "node_shift": noise(seeds[13], (D,), 0.3, 2.0, (), jnp.float32),
        "node_cot": noise(seeds[14], (SAMPLES, NODES, D), 1.0, 6.0, ((0, 2), (1, 16))),
        "edge_cot": noise(seeds[15], (SAMPLES, EDGES, D), 1.0, 6.0, ((0, 2), (1, 16))),
        "send_index": draw_send_index(jax.random.fold_in(seeds[20], 71), 0),
        "edge_sender": draw_edge_sender(jax.random.fold_in(seeds[20], 71), 0),
        "edge_receiver": draw_edge_receiver(jax.random.fold_in(seeds[20], 71), 0),
        "node_mask": draw_node_mask(jax.random.fold_in(seeds[20], 71), 0),
    }


EPS = 1e-05
PRECISE = lax.Precision.HIGHEST

@jax.custom_vjp
def low(v):
    return lax.optimization_barrier(v.astype(jnp.bfloat16)).astype(jnp.float32)

@jax.custom_vjp
def low_back(v):
    return v

def low_keep(v):
    return (low(v), None)

def low_pass(kept, grad):
    return (grad,)

def back_keep(v):
    return (v, None)

def back_low(kept, grad):
    return (low(grad),)
low.defvjp(low_keep, low_pass)
low_back.defvjp(back_keep, back_low)

def layer_norm(values, gain, shift):
    average = lax.optimization_barrier(jnp.mean(values, axis=-1, keepdims=True))
    centred = values - average
    spread = lax.optimization_barrier(jnp.mean(centred * centred, axis=-1, keepdims=True))
    return centred * lax.rsqrt(spread + EPS) * gain + shift

def branch(inputs, w_first, b_first, w_second, b_second, gain, shift):
    hidden = low_back(jnp.dot(inputs, w_first, precision=PRECISE) + b_first)
    active = low(jax.nn.silu(hidden))
    output = low_back(jnp.dot(active, w_second, precision=PRECISE) + b_second)
    return layer_norm(output, gain, shift)

def graph_rows(send_index, edge_sender, edge_receiver):
    blocks = jnp.arange(GRAPH_BLOCKS, dtype=jnp.int32)
    offsets = blocks * NODE_DEV
    near_ids = jnp.arange(NEAR, dtype=jnp.int32)
    shifts = near_ids - NEAR // 2 + (near_ids >= NEAR // 2).astype(jnp.int32)
    owners = jnp.mod(blocks[:, None] - shifts[None, :], GRAPH_BLOCKS).astype(jnp.int32)
    slot_table = send_index[owners, near_ids[None, :]] + (owners * NODE_DEV)[:, :, None]
    slot_table = slot_table.reshape(GRAPH_BLOCKS, NEAR * CAP).astype(jnp.int32)
    local_sender = edge_sender.reshape(GRAPH_BLOCKS, EDGE_DEV)
    halo_slot = jnp.clip(local_sender - NODE_DEV, 0, NEAR * CAP - 1).astype(jnp.int32)
    from_halo = jnp.take_along_axis(slot_table, halo_slot, axis=1)
    sender_rows = jnp.where(local_sender < NODE_DEV, local_sender + offsets[:, None], from_halo)
    receiver_rows = edge_receiver.reshape(GRAPH_BLOCKS, EDGE_DEV) + offsets[:, None]
    return (sender_rows.reshape(EDGES).astype(jnp.int32), receiver_rows.reshape(EDGES).astype(jnp.int32))

def reference(node_latents, edge_latents, edge_first, edge_first_bias, edge_second, edge_second_bias, edge_gain, edge_shift, node_first, node_first_bias, node_second, node_second_bias, node_gain, node_shift, node_cot, edge_cot, send_index, edge_sender, edge_receiver, node_mask):
    sender_rows, receiver_rows = graph_rows(send_index, edge_sender, edge_receiver)
    node_live = node_mask.astype(jnp.float32)[:, None]
    edge_live = jnp.take(node_live, receiver_rows, axis=0)
    params = tuple((weight.astype(jnp.float32) for weight in (edge_first, edge_first_bias, edge_second, edge_second_bias, edge_gain, edge_shift, node_first, node_first_bias, node_second, node_second_bias, node_gain, node_shift)))

    def forward(node_rows, edge_rows, weights):
        senders = jnp.take(node_rows, sender_rows, axis=0)
        receivers = jnp.take(node_rows, receiver_rows, axis=0)
        edge_inputs = jnp.concatenate([edge_rows, senders, receivers], axis=1)
        message = edge_live * branch(edge_inputs, weights[0], weights[1], weights[2], weights[3], weights[4], weights[5])
        gathered = low(jax.ops.segment_sum(message, receiver_rows, NODES))
        node_inputs = jnp.concatenate([node_rows, gathered], axis=1)
        update = node_live * branch(node_inputs, weights[6], weights[7], weights[8], weights[9], weights[10], weights[11])
        return (node_rows + update, edge_rows + message)

    def one_sample(totals, sample):
        node_rows, edge_rows, node_up, edge_up = sample
        outputs, pullback = jax.vjp(forward, node_rows.astype(jnp.float32), edge_rows.astype(jnp.float32), params)
        node_back, edge_back, param_grads = pullback((node_up.astype(jnp.float32), edge_up.astype(jnp.float32)))
        totals = jax.tree.map(jnp.add, totals, param_grads)
        return (totals, (outputs[0].astype(jnp.bfloat16), outputs[1].astype(jnp.bfloat16), node_back, edge_back.astype(jnp.bfloat16)))
    empty_sums = tuple((jnp.zeros(weight.shape, jnp.float32) for weight in params))
    totals, stacked = lax.scan(one_sample, empty_sums, (node_latents, edge_latents, node_cot, edge_cot))
    return (stacked[0], stacked[1], stacked[2], stacked[3], totals[0], totals[1], totals[2], totals[3], totals[4], totals[5], totals[6], totals[7], totals[8], totals[9], totals[10], totals[11])
```

```python
import functools

import jax
import jax.numpy as jnp
from jax import lax
from jax.experimental import pallas as pl
from jax.experimental.pallas import tpu as pltpu
from jax.sharding import PartitionSpec as P

EPS = 1e-05
VMEM = 60 * 1024 * 1024
BLOCK = 16
BATCH = 128
F32 = jnp.float32
BF16 = jnp.bfloat16


def dot(left, right):
    return jnp.dot(left, right, preferred_element_type=F32)


def dot_rows(left, right):
    return lax.dot_general(left, right, (((0,), (0,)), ((), ())), preferred_element_type=F32)


def dot_columns(left, right):
    return lax.dot_general(left, right, (((1,), (1,)), ((), ())), preferred_element_type=F32)


def fold(values):
    rows, width = values.shape
    return jnp.sum(values.reshape(rows // 8, 8, width), axis=0)


def logistic(values):
    return 0.5 * jnp.tanh(0.5 * values) + 0.5


def normalize(values):
    average = jnp.mean(values, axis=-1, keepdims=True)
    centred = values - average
    inverse = lax.rsqrt(jnp.mean(centred * centred, axis=-1, keepdims=True) + EPS)
    return centred * inverse, inverse


def norm_back(scaled, normed, inverse):
    average = jnp.mean(scaled, axis=-1, keepdims=True)
    along = jnp.mean(scaled * normed, axis=-1, keepdims=True)
    return inverse * (scaled - average - normed * along)


def lanes(values, width):
    return jnp.concatenate([values] * (width // values.shape[1]), axis=1)


def lane_parts(values):
    width = values.shape[1]
    return sum(values[:, at : at + 128] for at in range(128, width, 128)) + values[:, :128]


def row_sums(parts):
    return jnp.sum(jnp.concatenate(parts), axis=-1, keepdims=True)


def one_hot_columns(index_column, count):
    lanes = lax.broadcasted_iota(jnp.int32, (index_column.shape[0], count), 1).astype(F32)
    return jnp.where(index_column == lanes, 1.0, 0.0).astype(BF16)


def one_hot_rows(index_row, count):
    rows = lax.broadcasted_iota(jnp.int32, (count, index_row.shape[1]), 0).astype(F32)
    return jnp.where(index_row == rows, 1.0, 0.0).astype(BF16)


def edge_start(idx, x, nodes, first, vec, partial, inputs, table):
    tile, sample = pl.program_id(0), pl.program_id(1)
    width = x.shape[2]
    here = nodes.shape[1]

    @pl.when(tile == 0)
    def _():
        table[sample, :here] = (dot(nodes[sample], first[width : 2 * width]) * 0.5).astype(BF16)
        table[sample, here : 2 * here] = (
            (dot(nodes[sample], first[2 * width :]) + vec[0:1]) * 0.5
        ).astype(BF16)
        table[sample, 2 * here :] = first[:width] * 0.5

    @pl.when(sample == 0)
    def _():
        columns = idx[0].T
        inputs[:, :here] = one_hot_columns(columns[:, 0:1], here)
        inputs[:, here : 2 * here] = one_hot_columns(columns[:, 1:2], here)

    inputs[:, 2 * here :] = x[0]
    partial[0] = dot(inputs[...], table[sample]).astype(BF16)


def edge_forward(
    idx, count, partial, arrived, send, second, vec, node_vec,
    nodes_hbm, cot_hbm, node_first_hbm, node_second_hbm,
    act, bend, nrm, inv, vec_grad, nodes_out_hbm, base_hbm, gathered_grad_hbm, weight_grad_hbm,
    inputs, picks, table, live, degree, sums, node_inputs, node_actives, pre_grads, hidden_grads,
    projected, ordered, nodes, cot, node_first, node_second,
    nodes_out, base, gathered_grad, weight_grad, arrive, leave,
):
    tile, sample = pl.program_id(0), pl.program_id(1)
    samples, here, width = nodes.shape
    near = arrived.shape[0]
    slots = arrived.shape[1] // samples
    far = near * slots
    rows = partial.shape[1]
    chunk = rows // 4
    begin = (tile == 0) & (sample == 0)
    end = (tile == pl.num_programs(0) - 1) & (sample == samples - 1)
    incoming = [
        pltpu.make_async_copy(source, target, arrive.at[number])
        for number, (source, target) in enumerate(
            [
                (nodes_hbm, nodes),
                (cot_hbm, cot),
                (node_first_hbm, node_first),
                (node_second_hbm, node_second),
            ]
        )
    ]

    @pl.when(begin)
    def _():
        for copy in incoming:
            copy.start()
        foreign = arrived[...].reshape(samples * far, width)
        projected[...] = dot(foreign, send[...]) * 0.5
        sums[...] = jnp.zeros(sums.shape, F32)
        degree[...] = jnp.zeros(degree.shape, F32)
        table[...] = jnp.zeros(table.shape, BF16)
        for s in range(samples):
            for j in range(near):
                row = (j * samples + s) * slots
                ordered[j * slots : (j + 1) * slots] = projected[row : row + slots]
            table[s, :far] = ordered[...].astype(BF16)

    @pl.when(sample == 0)
    def _():
        columns = idx[0].T
        inputs[...] = one_hot_columns(columns[:, 0:1] - here, table.shape[1])
        live[...] = jnp.broadcast_to(columns[:, 2:3], live.shape)
        chosen = one_hot_rows(idx[0, 1:2], here)
        picks[...] = chosen
        counts = jnp.sum(chosen.astype(F32), axis=-1, keepdims=True)
        degree[...] += jnp.broadcast_to(counts, degree.shape)

    picked, pres = {}, {}

    def pick(number):
        at = slice(number * chunk, (number + 1) * chunk)
        picked[number] = dot(inputs[at], table[sample])

    def activate(number):
        for row in range(0, chunk, BLOCK):
            at = slice(number * chunk + row, number * chunk + row + BLOCK)
            value = partial[0, at].astype(F32) + picked[number][row : row + BLOCK]
            bent = jnp.tanh(value)
            twice = bent + 1.0
            silu = value * twice
            act[0, at] = silu.astype(BF16)
            bend[0, at] = (twice + silu * (1.0 - bent)).astype(BF16)
        pres[number] = dot(act[0, number * chunk : (number + 1) * chunk], second[...])

    def finish(number):
        for first_row in range(0, chunk, chunk // 2):
            batch = range(first_row, first_row + chunk // 2, BLOCK)
            values = [pres[number][row : row + BLOCK] + vec[1:2] for row in batch]
            average = row_sums([lane_parts(value) for value in values]) * (1.0 / width)
            centred = [
                value - average[n * BLOCK : (n + 1) * BLOCK] for n, value in enumerate(values)
            ]
            spread = row_sums([lane_parts(value * value) for value in centred]) * (1.0 / width)
            inverse = lax.rsqrt(spread + EPS)
            for n, row in enumerate(batch):
                at = slice(number * chunk + row, number * chunk + row + BLOCK)
                scale = inverse[n * BLOCK : (n + 1) * BLOCK] * live[at]
                nrm[0, at] = (centred[n] * lanes(scale, width)).astype(BF16)
                inv[0, at] = scale

    stages = (pick, activate, finish)
    for turn in range(4 + len(stages) - 1):
        for stage in reversed(range(len(stages))):
            if 0 <= turn - stage < 4:
                stages[stage](turn - stage)
    sums[sample] += dot(picks[...], nrm[0])

    @pl.when(end)
    def _():
        for copy in incoming:
            copy.wait()
        lines = lax.broadcasted_iota(jnp.int32, (here, 1), 0)
        alive = jnp.where(lines < count[0], 1.0, 0.0)
        shifts = lanes(degree[...], width) * vec[3:4]
        vectors = [jnp.zeros((8, width), F32) for _ in range(4)]
        hidden, pre, back = {}, {}, {}

        def first_layer(s):
            at = slice(s * here, (s + 1) * here)
            node_inputs[at, :width] = nodes[s]
            node_inputs[at, width:] = (sums[s] * vec[2:3] + shifts).astype(BF16)
            hidden[s] = dot(node_inputs[at], node_first[...])

        def second_layer(s):
            for row in range(0, here, BLOCK):
                at = slice(s * here + row, s * here + row + BLOCK)
                value = hidden[s][row : row + BLOCK] + node_vec[0:1]
                node_actives[at] = (value * logistic(value)).astype(BF16)
            pre[s] = dot(node_actives[s * here : (s + 1) * here], node_second[...])

        def norm(s):
            for row in range(0, here, BLOCK):
                inside = slice(row, row + BLOCK)
                normed, inverse = normalize(pre[s][inside] + node_vec[1:2])
                update = alive[inside] * (normed * node_vec[2:3] + node_vec[3:4])
                nodes_out[s, inside] = (nodes[s, inside].astype(F32) + update).astype(BF16)
                out_grad = alive[inside] * cot[s, inside].astype(F32)
                vectors[2] += fold(out_grad * normed)
                vectors[3] += fold(out_grad)
                pre_grad = norm_back(out_grad * node_vec[2:3], normed, inverse)
                vectors[1] += fold(pre_grad)
                pre_grads[s * here + row : s * here + row + BLOCK] = pre_grad.astype(BF16)
            pltpu.make_async_copy(nodes_out.at[s], nodes_out_hbm.at[s], leave.at[s]).start()
            back[s] = dot_columns(pre_grads[s * here : (s + 1) * here], node_second[...])

        def first_back(s):
            for row in range(0, here, BLOCK):
                at = slice(s * here + row, s * here + row + BLOCK)
                value = hidden[s][row : row + BLOCK] + node_vec[0:1]
                sigma = logistic(value)
                hidden_grad = back[s][row : row + BLOCK] * (sigma + value * sigma * (1.0 - sigma))
                vectors[0] += fold(hidden_grad)
                hidden_grads[at] = hidden_grad.astype(BF16)
            down = dot_columns(hidden_grads[s * here : (s + 1) * here], node_first[...])
            base[s] = cot[s].astype(F32) + down[:, :width]
            gathered_grad[s] = down[:, width:].astype(BF16)
            for number, (source, target) in enumerate(
                [(gathered_grad, gathered_grad_hbm), (base, base_hbm)]
            ):
                pltpu.make_async_copy(
                    source.at[s], target.at[s], leave.at[samples * (1 + number) + s]
                ).start()

        steps = (first_layer, second_layer, norm, first_back)
        for turn in range(samples + len(steps) - 1):
            for stage in reversed(range(len(steps))):
                if 0 <= turn - stage < samples:
                    steps[stage](turn - stage)
        weight_grad[: 2 * width] = dot_rows(node_inputs[...], hidden_grads[...]).astype(BF16)
        weight_grad[2 * width :] = dot_rows(node_actives[...], pre_grads[...]).astype(BF16)
        weights = pltpu.make_async_copy(weight_grad, weight_grad_hbm, leave.at[3 * samples])
        weights.start()
        for number in range(4):
            vec_grad[number] = vectors[number]
        for number, (source, target) in enumerate(
            [(nodes_out, nodes_out_hbm), (gathered_grad, gathered_grad_hbm), (base, base_hbm)]
        ):
            for s in range(samples):
                pltpu.make_async_copy(
                    source.at[s], target.at[s], leave.at[samples * number + s]
                ).wait()
        weights.wait()


def edge_backward(
    idx, early, late, cot, act, late_act, bend, nrm, inv, up, second, vec,
    x_hbm, act_hbm, send_hbm,
    hidden_out, vec_grad, local_hbm, remote_hbm, received_hbm, outbound_hbm, weight_grad_hbm,
    picks, narrow_picks, spread_a, spread_b, turned, pre_a, pre_b, hid_a, hid_b, dead_rows, flags,
    second_t, sums, first_grad, second_grad, ordered,
    final, final_act, send, local, remote, received, outbound, weight_grad, arrive, leave,
):
    step = pl.program_id(0)
    last = pl.num_programs(0) - 1
    samples, here, width = local.shape
    near = outbound.shape[0]
    slots = outbound.shape[1] // samples
    far = near * slots
    senders = here + far
    rows = early.shape[1]
    edges = x_hbm.shape[1]
    pairs = samples // 2
    window = narrow_picks.shape[1]
    pair = step % pairs
    before = 2 * (jnp.maximum(step - 1, 0) % pairs) + 1
    incoming = [
        pltpu.make_async_copy(source, target, arrive.at[number])
        for number, (source, target) in enumerate(
            [
                (x_hbm.at[samples - 1, pl.ds(edges - rows, rows)], final),
                (act_hbm.at[samples - 1, pl.ds(edges - rows, rows)], final_act),
                (send_hbm.at[pl.ds(width, width)], send),
            ]
        )
    ]

    @pl.when(step == 0)
    def _():
        for copy in incoming:
            copy.start()
        first_grad[...] = jnp.zeros(first_grad.shape, F32)
        second_grad[...] = jnp.zeros(second_grad.shape, F32)
        vec_grad[...] = jnp.zeros(vec_grad.shape, F32)
        sums[...] = jnp.zeros(sums.shape, F32)
        turned[width:] = jnp.ones((BLOCK, rows), BF16)
        pre_b[...] = jnp.zeros(pre_b.shape, BF16)
        hid_b[...] = jnp.zeros(hid_b.shape, BF16)
        spread_b[...] = jnp.zeros(spread_b.shape, BF16)
        second_t[...] = (second[...] * 0.5).T

    @pl.when(pair == 0)
    def _():
        receivers = idx[0, 1:2]
        lowest = jnp.min(jnp.where(receivers < 0.0, float(here), receivers)).astype(jnp.int32)
        highest = jnp.max(receivers).astype(jnp.int32)
        start = jnp.minimum(lowest // 16 * 16, here - window)
        flags[0] = (jnp.min(idx[0, 2:3]) < 0.5).astype(jnp.int32)
        flags[1] = (highest < start + window).astype(jnp.int32)
        flags[2] = start
        columns = idx[0].T[:, 1:2]
        picks[...] = one_hot_columns(columns, here)
        narrow_picks[...] = one_hot_columns(columns - start.astype(F32), window)
        dead_rows[...] = jnp.broadcast_to(1.0 - idx[0, 2:3], dead_rows.shape).astype(BF16)
        spread_a[:senders] = one_hot_rows(idx[0, 0:1], senders)
        spread_a[senders:] = one_hot_rows(idx[0, 1:2], here)

    @pl.when(pair == 1)
    def _():
        spread_b[...] = spread_a[...]

    def outer(act, pre):
        def piece(columns):
            if columns.start == 0:
                turned[:width] = act.T
            second_grad[:, columns] += dot(turned[...], pre[:, columns])

        return [lambda at=at: piece(at) for at in sides]

    def input_outer(x, hid):
        transposed = {}

        def piece(columns):
            if not transposed:
                transposed[0] = x.T
            first_grad[:, columns] += dot(transposed[0], hid[:, columns])

        return [lambda at=at: piece(at) for at in sides]

    def scatter(spread, hid, where):
        def piece(columns):
            sums[where, :, columns] += dot(spread[...], hid[:, columns])

        return [lambda at=at: piece(at) for at in sides]

    sides = [slice(0, width // 2), slice(width // 2, width)]

    def main(narrow):
        sums_at = [jnp.zeros((8, width), F32) for _ in range(2)]
        results = {}

        def norm_part(side, pre, first_row):
            batch = range(first_row, first_row + BATCH, BLOCK)
            kept, averages, slopes = [], [], []
            for row in batch:
                at = slice(row, row + BLOCK)
                normed = nrm[side, at].astype(F32)
                scaled = (cot[side, at].astype(F32) + results[side][at]) * vec[2:3]
                along = scaled * normed
                sums_at[0] += fold(along)
                sums_at[1] += fold(scaled)
                kept.append(scaled)
                averages.append(lane_parts(scaled))
                slopes.append(lane_parts(along))
            average = row_sums(averages) * (1.0 / width)
            slope = row_sums(slopes) * (1.0 / width)
            for n, row in enumerate(batch):
                at = slice(row, row + BLOCK)
                inside = slice(n * BLOCK, (n + 1) * BLOCK)
                change = kept[n] - average[inside] - slope[inside] * nrm[side, at].astype(F32)
                pre[at] = (change * lanes(inv[side, at], width)).astype(BF16)

        def silu_part(side, hid, first_row):
            for row in range(first_row, first_row + BATCH, BLOCK):
                at = slice(row, row + BLOCK)
                hidden_grad = (results[2 + side][at] * bend[side, at].astype(F32)).astype(BF16)
                hid[at] = hidden_grad
                hidden_out[side, at] = hidden_grad

        def interleave(part, pieces):
            batches = range(0, rows, BATCH)
            spots = [len(batches) * n // len(pieces) for n in range(len(pieces))]
            for number, row in enumerate(batches):
                while spots and number == spots[0]:
                    spots.pop(0)
                    pieces.pop(0)()
                part(row)

        def pick(side):
            if narrow:
                some = up[side, pl.ds(pl.multiple_of(flags[2], 16), window)]
                results[side] = dot(narrow_picks[...], some)
            else:
                results[side] = dot(picks[...], up[side])

        def back(side, pre):
            results[2 + side] = dot(pre[...], second_t[...])

        pick(0)
        interleave(
            lambda row: norm_part(0, pre_a, row),
            [lambda: pick(1)] + outer(late_act[0], pre_b),
        )
        interleave(
            lambda row: norm_part(1, pre_b, row),
            [lambda: back(0, pre_a)] + input_outer(late[0], hid_b),
        )
        interleave(
            lambda row: silu_part(0, hid_a, row),
            [lambda: back(1, pre_b)] + scatter(spread_b, hid_b, before),
        )
        interleave(
            lambda row: silu_part(1, hid_b, row),
            outer(act[0], pre_a)
            + input_outer(early[0], hid_a)
            + scatter(spread_a, hid_a, 2 * pair),
        )
        for number in range(2):
            vec_grad[2 + number] += sums_at[number]

    @pl.when(flags[1] == 1)
    def _():
        main(True)

    @pl.when(flags[1] == 0)
    def _():
        main(False)

    @pl.when(flags[0] == 1)
    def _():
        extra = dot(dead_rows[...], cot[0]) + dot(dead_rows[...], cot[1])
        vec_grad[3] -= extra[:8] * 0.125 * vec[2:3]

    @pl.when(step == last)
    def _():
        leaving = []

        def send_off(source, target):
            copy = pltpu.make_async_copy(source, target, leave.at[len(leaving)])
            copy.start()
            leaving.append(copy)

        def part(number):
            return pl.ds(number * width, width)

        for copy in incoming:
            copy.wait()
        for piece in outer(final_act[...], pre_b):
            piece()
        weight_grad[3 * width :] = second_grad[:width].astype(BF16)
        vec_grad[1] = second_grad[width : width + 8] * 0.125
        send_off(weight_grad.at[part(3)], weight_grad_hbm.at[part(3)])
        for piece in input_outer(final[...], hid_b) + scatter(spread_b, hid_b, samples - 1):
            piece()
        weight_grad[:width] = first_grad[...].astype(BF16)
        send_off(weight_grad.at[part(0)], weight_grad_hbm.at[part(0)])
        for s in range(samples):
            for j in range(near):
                row, place = here + j * slots, (j * samples + s) * slots
                ordered[place : place + slots] = sums[s, row : row + slots]
        remote[...] = ordered[...].astype(BF16)
        outbound[...] = dot_columns(remote[...], send[...]).astype(BF16).reshape(outbound.shape)
        send_off(outbound, outbound_hbm)
        send_off(remote, remote_hbm)
        local[...] = sums[:, :here].astype(BF16)
        send_off(local, local_hbm)
        received[...] = sums[:, senders:].astype(BF16)
        send_off(received, received_hbm)
        every = jnp.zeros((8, width), F32)
        for s in range(samples):
            every += fold(sums[s, :senders])
        vec_grad[0] = every
        for number in (2, 3):
            vec_grad[number] = vec_grad[number] / vec[2:3]
        for copy in leaving:
            copy.wait()


def edge_totals(
    local, received, remote, nodes, arrived, base, first, weights_in, after,
    node_grad, weights, made, leave,
):
    samples, here, width = nodes.shape
    owned = nodes[...].reshape(samples * here, width)
    mine = local[...].reshape(samples * here, width)
    got = received[...].reshape(samples * here, width)
    foreign = arrived[...].reshape(remote.shape)
    made[:width] = (dot_rows(owned, mine) + dot_rows(foreign, remote[...])).astype(BF16)
    made[width:] = dot_rows(owned, got).astype(BF16)
    copy = pltpu.make_async_copy(made, weights.at[pl.ds(width, 2 * width)], leave)
    copy.start()
    grads = dot_columns(mine, first[width : 2 * width]) + dot_columns(got, first[2 * width :])
    node_grad[...] = base[...] + grads.reshape(node_grad.shape)
    copy.wait()


def edge_outputs(idx, x_low, x_high, nrm_low, nrm_high, vec, after, edges_out, live):
    @pl.when(pl.program_id(1) == 0)
    def _():
        live[...] = jnp.broadcast_to(idx[0].T[:, 2:3], live.shape)

    rows = x_low.shape[1]
    for start, x, nrm in ((0, x_low, nrm_low), (rows, x_high, nrm_high)):
        for row in range(0, rows, BLOCK):
            inside = slice(row, row + BLOCK)
            at = slice(start + row, start + row + BLOCK)
            message = nrm[0, inside].astype(F32) * vec[2:3] + vec[3:4]
            message = jnp.where(lanes(live[at], message.shape[1]) > 0.0, message, 0.0)
            edges_out[0, at] = (x[0, inside].astype(F32) + message).astype(BF16)


def edge_gradient(cot_low, cot_high, hid_low, hid_high, first, after, edge_grad, first_t):
    @pl.when((pl.program_id(0) == 0) & (pl.program_id(1) == 0))
    def _():
        first_t[...] = first[...].T

    rows = cot_low.shape[1]
    for start, cot, hid in ((0, cot_low, hid_low), (rows, cot_high, hid_high)):
        at = slice(start, start + rows)
        edge_grad[0, at] = (cot[0].astype(F32) + dot(hid[0], first_t[...])).astype(BF16)


def unpack(totals, *refs):
    outs, (taken, given, arrive, leave) = refs[:-4], refs[-4:]
    rows = taken.shape[1]
    width = totals.shape[2]
    edge_half, node_half = 2 * width, (totals.shape[1] - 2 * width) // rows * rows
    places = []
    for core in range(2):
        for start, count, pair in ((0, edge_half, outs[:2]), (edge_half, node_half, outs[2:])):
            for row in range(0, count, rows):
                goal = core * count + row
                if goal < pair[0].shape[0]:
                    places.append((core, start + row, pair[0], goal))
                else:
                    places.append((core, start + row, pair[1], goal - pair[0].shape[0]))
    incoming = [
        pltpu.make_async_copy(totals.at[core, pl.ds(row, rows)], taken.at[n], arrive.at[n])
        for n, (core, row, _, _) in enumerate(places)
    ]
    leaving = [
        pltpu.make_async_copy(given.at[n], goal.at[pl.ds(row, rows)], leave.at[n])
        for n, (_, _, goal, row) in enumerate(places)
    ]
    for copy in incoming:
        copy.start()
    for n in range(len(places)):
        incoming[n].wait()
        given[n] = taken[n].astype(F32)
        leaving[n].start()
    for copy in leaving:
        copy.wait()


def whole(shape):
    return pl.BlockSpec(
        shape, lambda *_: (0,) * len(shape), pipeline_mode=pl.Buffered(buffer_count=1)
    )


def unread():
    return pl.BlockSpec(memory_space=pl.ANY)


def params(steps):
    return pltpu.CompilerParams(
        dimension_semantics=("arbitrary",) * steps, vmem_limit_bytes=VMEM
    )


def peer_offset(number, near):
    half = near // 2
    return number - half if number < half else number - half + 1


def shift(block, distance):
    size = lax.axis_size("graph")
    return lax.ppermute(block, "graph", [(i, (i + distance) % size) for i in range(size)])


def all_peers(near):
    return lax.axis_size("graph") == near


def exchange(chunks, sign):
    near = chunks.shape[0]
    if not all_peers(near):
        return jnp.stack([shift(chunks[j], sign * peer_offset(j, near)) for j in range(near)])
    me = lax.axis_index("graph")
    swapped = lax.all_to_all(chunks, "graph", 0, 0)
    own = lax.dynamic_index_in_dim(chunks, me, 0, keepdims=False)
    opposite = shift(own, near // 2)
    mine = (jnp.arange(near) == me)[:, None, None]
    return jnp.where(mine, opposite[None], swapped)


def chunk_order(send_index):
    near = send_index.shape[0]
    if not all_peers(near):
        return send_index
    numbers = jnp.arange(near, dtype=jnp.int32)
    distance = (numbers - lax.axis_index("graph") + near) % near
    number = jnp.where(distance <= near // 2, distance + near // 2 - 1, distance - near // 2)
    number = jnp.where(distance == 0, 0, number)
    chosen = number[:, None, None] == numbers[None, :, None]
    return jnp.sum(jnp.where(chosen, send_index[None], 0), axis=1)


def chunk_rows(edge_sender, here, near, slots):
    if not all_peers(near):
        return edge_sender
    slot = edge_sender - here
    number = slot // slots
    offset = number - near // 2 + (number >= near // 2).astype(jnp.int32)
    offset = jnp.where(number == 0, 0, offset)
    owner = (lax.axis_index("graph") - offset + near) % near
    return jnp.where(slot < 0, edge_sender, here + owner * slots + slot % slots)


def rounded(values):
    return lax.reduce_precision(values, 8, 7)


def split_rows(vectors):
    high = rounded(vectors)
    return jnp.concatenate([high, rounded(vectors - high)])


def repeat(block, count):
    return jnp.broadcast_to(block[None], (count,) + block.shape)


def scatter_all(grads):
    rows, width = grads.shape
    parts = 2 * lax.axis_size("graph")
    return lax.all_to_all(grads.reshape(parts, rows // parts, width), ("dp", "graph"), 0, 0)


def add_parts(parts):
    return jnp.sum(parts.astype(F32), axis=0)


def side_groups():
    size = lax.axis_size("graph")
    return [list(range(size // 2)), list(range(size // 2, size))]


def swap_sides(block):
    return shift(block, lax.axis_size("graph") // 2)


def both_sides(piece, other):
    size = lax.axis_size("graph")
    low = lax.axis_index("graph") < size // 2
    return jnp.concatenate([jnp.where(low, piece, other), jnp.where(low, other, piece)])


def exchange_in_side(pieces):
    return lax.all_to_all(pieces, "graph", 0, 0, axis_index_groups=side_groups())


def gather_cores(block):
    return lax.all_to_all(repeat(block, 2), "dp", 0, 0)


def pair_pieces(grads, vectors):
    rows, width = grads.shape
    size = lax.axis_size("graph") // 2
    half = rows // 2
    core = lax.axis_index("dp")
    leaving = lax.dynamic_slice_in_dim(grads, (1 - core) * half, half)
    other = lax.ppermute(leaving, "dp", [(0, 1), (1, 0)])
    mine = lax.dynamic_slice_in_dim(grads, core * half, half)
    pieces = (mine.astype(F32) + other.astype(F32)).astype(BF16)
    pieces = pieces.reshape(size, half // size, width)
    return jnp.concatenate([pieces, repeat(split_rows(vectors).astype(BF16), size)], axis=1)


def shards(
    node_latents,
    edge_latents,
    edge_first,
    edge_first_bias,
    edge_second,
    edge_second_bias,
    edge_gain,
    edge_shift,
    node_first,
    node_first_bias,
    node_second,
    node_second_bias,
    node_gain,
    node_shift,
    node_cot,
    edge_cot,
    send_index,
    edge_sender,
    edge_receiver,
    node_mask,
):
    samples, here, width = node_latents.shape
    edges = edge_latents.shape[1]
    near, slots = send_index.shape[1:]
    far = near * slots
    senders = here + far

    targets = chunk_order(send_index[0])
    targets = targets[:, None, :] + here * jnp.arange(samples, dtype=jnp.int32)[None, :, None]
    pick = jax.nn.one_hot(targets.reshape(-1), samples * here, dtype=BF16)
    parcels = dot(pick, node_latents.reshape(samples * here, width)).astype(BF16)
    arrived = exchange(parcels.reshape(near, samples * slots, width), 1)

    edge_live = edge_receiver < here - 1
    idx = jnp.stack(
        [
            chunk_rows(edge_sender, here, near, slots).astype(F32),
            jnp.where(edge_live, edge_receiver, -1).astype(F32),
            edge_live.astype(F32),
        ]
    )
    idx = jnp.pad(idx, ((0, 5), (0, 0)))
    zero = jnp.zeros((width,), F32)
    edge_vec = jnp.stack(
        [edge_first_bias, edge_second_bias, edge_gain, edge_shift, zero, zero, zero, zero]
    )
    node_vec = jnp.stack(
        [node_first_bias, node_second_bias, node_gain, node_shift, zero, zero, zero, zero]
    )
    unit = 2 * samples * edges * width * width

    def third(number):
        return pl.BlockSpec(
            (width, width), lambda *_: (number, 0), pipeline_mode=pl.Buffered(buffer_count=1)
        )

    edge_shape = jax.ShapeDtypeStruct((samples, edges, width), BF16)
    inv_shape = jax.ShapeDtypeStruct((samples, edges, 128), F32)
    node_shape = jax.ShapeDtypeStruct((samples, here, width), BF16)
    node_sums_shape = jax.ShapeDtypeStruct((samples, here, width), F32)
    vec_shape = jax.ShapeDtypeStruct((4, 8, width), F32)

    def edge_block(rows):
        return pl.BlockSpec((1, rows, width), lambda t, s: (s, t, 0))

    def two_halves(rows):
        return [
            pl.BlockSpec((1, rows // 2, width), lambda t, s, n=n: (s, 2 * t + n, 0))
            for n in range(2)
        ]

    def idx_block(rows):
        return pl.BlockSpec((1, 8, rows), lambda t, s: (t, 0, 0))

    def inv_block(rows):
        return pl.BlockSpec((1, rows, 128), lambda t, s: (s, t, 0))

    def tiled(rows):
        return idx.reshape(8, edges // rows, rows).transpose(1, 0, 2)

    wide = edges // 2
    partial = pl.pallas_call(
        edge_start,
        grid=(edges // wide, samples),
        in_specs=[
            idx_block(wide),
            edge_block(wide),
            whole((samples, here, width)),
            whole((3 * width, width)),
            whole((8, width)),
        ],
        out_specs=edge_block(wide),
        out_shape=edge_shape,
        scratch_shapes=[
            pltpu.VMEM((wide, 2 * here + width), BF16),
            pltpu.VMEM((samples, 2 * here + width, width), BF16),
        ],
        compiler_params=params(2),
        cost_estimate=pl.CostEstimate(
            flops=3 * unit, bytes_accessed=4 * samples * edges * width, transcendentals=0
        ),
        name="edge_start",
    )(tiled(wide), edge_latents, node_latents, edge_first, edge_vec)

    count = jnp.sum(node_mask).reshape(1)
    remote = -(-far // 128) * 128
    (
        act, bend, nrm, inv, node_sums, nodes_out, base, gathered_grad, node_weights
    ) = pl.pallas_call(
        edge_forward,
        grid=(edges // wide, samples),
        in_specs=[
            idx_block(wide),
            pl.BlockSpec(memory_space=pltpu.SMEM),
            edge_block(wide),
            whole((near, samples * slots, width)),
            third(1),
            whole((width, width)),
            whole((8, width)),
            whole((8, width)),
        ]
        + [unread()] * 4,
        out_specs=[edge_block(wide)] * 3
        + [inv_block(wide), whole((4, 8, width))]
        + [unread()] * 4,
        out_shape=[
            edge_shape,
            edge_shape,
            edge_shape,
            inv_shape,
            vec_shape,
            node_shape,
            node_sums_shape,
            node_shape,
            jax.ShapeDtypeStruct((3 * width, width), BF16),
        ],
        scratch_shapes=[
            pltpu.VMEM((wide, remote), BF16),
            pltpu.VMEM((here, wide), BF16),
            pltpu.VMEM((samples, remote, width), BF16),
            pltpu.VMEM((wide, 128), F32),
            pltpu.VMEM((here, 128), F32),
            pltpu.VMEM((samples, here, width), F32),
            pltpu.VMEM((samples * here, 2 * width), BF16),
            pltpu.VMEM((samples * here, width), BF16),
            pltpu.VMEM((samples * here, width), BF16),
            pltpu.VMEM((samples * here, width), BF16),
            pltpu.VMEM((samples * far, width), F32),
            pltpu.VMEM((far, width), F32),
            pltpu.VMEM((samples, here, width), BF16),
            pltpu.VMEM((samples, here, width), BF16),
            pltpu.VMEM((2 * width, width), BF16),
            pltpu.VMEM((width, width), BF16),
            pltpu.VMEM((samples, here, width), BF16),
            pltpu.VMEM((samples, here, width), F32),
            pltpu.VMEM((samples, here, width), BF16),
            pltpu.VMEM((3 * width, width), BF16),
            pltpu.SemaphoreType.DMA((4,)),
            pltpu.SemaphoreType.DMA((3 * samples + 1,)),
        ],
        compiler_params=params(2),
        cost_estimate=pl.CostEstimate(
            flops=4 * unit, bytes_accessed=8 * samples * edges * width, transcendentals=0
        ),
        name="edge_forward",
    )(
        tiled(wide), count, partial, arrived, edge_first, edge_second, edge_vec, node_vec,
        node_latents, node_cot, node_first, node_second,
    )
    node_parts = scatter_all(node_weights)

    short = edges // 5
    pairs = samples // 2

    def paired(lanes_here):
        return pl.BlockSpec((2, short, lanes_here), lambda i: (i % pairs, i // pairs, 0))

    def early_half(i):
        return (2 * (i % pairs), i // pairs, 0)

    def late_half(i):
        j = jnp.maximum(i - 1, 0)
        return (2 * (j % pairs) + 1, j // pairs, 0)

    (
        hidden_grad, edge_sums, local, remote_sums, received, outbound, edge_weights
    ) = pl.pallas_call(
        edge_backward,
        grid=(edges // short * pairs,),
        in_specs=[
            pl.BlockSpec((1, 8, short), lambda i: (i // pairs, 0, 0)),
            pl.BlockSpec((1, short, width), early_half),
            pl.BlockSpec((1, short, width), late_half),
            paired(width),
            pl.BlockSpec((1, short, width), early_half),
            pl.BlockSpec((1, short, width), late_half),
            paired(width),
            paired(width),
            paired(128),
            pl.BlockSpec((2, here, width), lambda i: (i % pairs, 0, 0)),
            whole((width, width)),
            whole((8, width)),
        ]
        + [unread()] * 3,
        out_specs=[paired(width), whole((4, 8, width))] + [unread()] * 5,
        out_shape=[
            edge_shape,
            vec_shape,
            node_shape,
            jax.ShapeDtypeStruct((samples * far, width), BF16),
            node_shape,
            jax.ShapeDtypeStruct((near, samples * slots, width), BF16),
            jax.ShapeDtypeStruct((4 * width, width), BF16),
        ],
        scratch_shapes=[
            pltpu.VMEM((short, here), BF16),
            pltpu.VMEM((short, min(256, here)), BF16),
            pltpu.VMEM((senders + here, short), BF16),
            pltpu.VMEM((senders + here, short), BF16),
            pltpu.VMEM((width + BLOCK, short), BF16),
            pltpu.VMEM((short, width), BF16),
            pltpu.VMEM((short, width), BF16),
            pltpu.VMEM((short, width), BF16),
            pltpu.VMEM((short, width), BF16),
            pltpu.VMEM((BLOCK, short), BF16),
            pltpu.SMEM((3,), jnp.int32),
            pltpu.VMEM((width, width), BF16),
            pltpu.VMEM((samples, senders + here, width), F32),
            pltpu.VMEM((width, width), F32),
            pltpu.VMEM((width + BLOCK, width), F32),
            pltpu.VMEM((samples * far, width), F32),
            pltpu.VMEM((short, width), BF16),
            pltpu.VMEM((short, width), BF16),
            pltpu.VMEM((width, width), BF16),
            pltpu.VMEM((samples, here, width), BF16),
            pltpu.VMEM((samples * far, width), BF16),
            pltpu.VMEM((samples, here, width), BF16),
            pltpu.VMEM((near, samples * slots, width), BF16),
            pltpu.VMEM((4 * width, width), BF16),
            pltpu.SemaphoreType.DMA((3,)),
            pltpu.SemaphoreType.DMA((6,)),
        ],
        compiler_params=params(1),
        cost_estimate=pl.CostEstimate(
            flops=7 * unit, bytes_accessed=10 * samples * edges * width, transcendentals=0
        ),
        name="edge_backward",
    )(
        tiled(short), edge_latents, edge_latents, edge_cot, act, act, bend, nrm, inv,
        gathered_grad, edge_second, edge_vec,
        edge_latents, act, edge_first,
    )
    node_parts, edge_weights, outbound = lax.optimization_barrier(
        (node_parts, edge_weights, outbound)
    )
    returned = exchange(outbound, -1)
    node_partial, edge_weights = pl.pallas_call(
        edge_totals,
        in_specs=[
            whole((samples, here, width)),
            whole((samples, here, width)),
            whole((samples * far, width)),
            whole((samples, here, width)),
            whole((near, samples * slots, width)),
            whole((samples, here, width)),
            whole((3 * width, width)),
            unread(),
            unread(),
        ],
        out_specs=[whole((samples, here, width)), unread()],
        out_shape=[node_sums_shape, jax.ShapeDtypeStruct((4 * width, width), BF16)],
        input_output_aliases={7: 1},
        scratch_shapes=[pltpu.VMEM((2 * width, width), BF16), pltpu.SemaphoreType.DMA],
        compiler_params=pltpu.CompilerParams(vmem_limit_bytes=VMEM),
        name="edge_totals",
    )(
        local, received, remote_sums, node_latents, arrived, base, edge_first, edge_weights,
        outbound,
    )
    vectors = jnp.concatenate([edge_sums, node_sums]).sum(axis=1)
    count = vectors.shape[0]
    pieces = pair_pieces(edge_weights, vectors)
    node_piece = add_parts(node_parts).astype(BF16)
    pieces, returned, node_piece = lax.optimization_barrier((pieces, returned, node_piece))
    arrived_pieces = exchange_in_side(pieces)
    edge_grad = pl.pallas_call(
        edge_gradient,
        grid=(edges // wide, samples),
        in_specs=[*two_halves(wide), *two_halves(wide), third(0), unread()],
        out_specs=edge_block(wide),
        out_shape=edge_shape,
        scratch_shapes=[pltpu.VMEM((width, width), BF16)],
        compiler_params=params(2),
        cost_estimate=pl.CostEstimate(
            flops=unit, bytes_accessed=6 * samples * edges * width, transcendentals=0
        ),
        name="edge_gradient",
    )(edge_cot, edge_cot, hidden_grad, hidden_grad, edge_first, pieces)
    arrived_pieces, edge_grad = lax.optimization_barrier((arrived_pieces, edge_grad))
    partial_sums = add_parts(arrived_pieces)
    piece = partial_sums.shape[0] - 2 * count
    vectors = split_rows(partial_sums[piece : piece + count] + partial_sums[piece + count :])
    partial_sums = jnp.concatenate([rounded(partial_sums[:piece]), vectors])
    other = swap_sides(jnp.concatenate([partial_sums.astype(BF16), node_piece]))
    totals = partial_sums + other[: piece + 2 * count].astype(F32)
    node_pair = both_sides(node_piece, other[piece + 2 * count :])
    vectors = totals[piece : piece + count] + totals[piece + count :]
    joined = jnp.concatenate([totals[:piece].astype(BF16), node_pair])
    gathered_rows = exchange_in_side(repeat(joined, lax.axis_size("graph") // 2))
    edges_out = pl.pallas_call(
        edge_outputs,
        grid=(edges // wide, samples),
        in_specs=[
            idx_block(wide),
            *two_halves(wide),
            *two_halves(wide),
            whole((8, width)),
            unread(),
        ],
        out_specs=edge_block(wide),
        out_shape=edge_shape,
        scratch_shapes=[pltpu.VMEM((wide, 128), F32)],
        compiler_params=params(2),
        cost_estimate=pl.CostEstimate(
            flops=0, bytes_accessed=6 * samples * edges * width, transcendentals=0
        ),
        name="edge_outputs",
    )(
        tiled(wide), edge_latents, edge_latents, nrm, nrm, edge_vec, joined,
    )
    gathered_rows, edges_out = lax.optimization_barrier((gathered_rows, edges_out))
    nodes_rows = gathered_rows[:, piece:]
    nodes_rows = nodes_rows.reshape(nodes_rows.shape[0], 2, -1, width).transpose(1, 0, 2, 3)
    halves = [
        gathered_rows[:, :piece].reshape(2 * width, width),
        nodes_rows.reshape(-1, width),
    ]
    totals = gather_cores(jnp.concatenate(halves + [split_rows(vectors).astype(BF16)]))
    chunk = width // 2
    parts = 7 * width // chunk
    weights = pl.pallas_call(
        unpack,
        in_specs=[unread()],
        out_specs=[unread()] * 4,
        out_shape=[
            jax.ShapeDtypeStruct((rows * width, width), F32) for rows in (3, 1, 2, 1)
        ],
        scratch_shapes=[
            pltpu.VMEM((parts, chunk, width), BF16),
            pltpu.VMEM((parts, chunk, width), F32),
            pltpu.SemaphoreType.DMA((parts,)),
            pltpu.SemaphoreType.DMA((parts,)),
        ],
        compiler_params=pltpu.CompilerParams(vmem_limit_bytes=VMEM),
        name="unpack",
    )(totals)
    vectors = totals[:, -2 * count :].astype(F32).sum(axis=0)
    vectors = vectors[:count] + vectors[count:]

    node_grad = node_partial + dot_rows(pick, returned.reshape(-1, width)).reshape(
        samples, here, width
    )
    return (
        nodes_out,
        edges_out,
        node_grad,
        edge_grad,
        weights[0],
        vectors[0],
        weights[1],
        vectors[1],
        vectors[2],
        vectors[3],
        weights[2],
        vectors[4],
        weights[3],
        vectors[5],
        vectors[6],
        vectors[7],
    )


def solution(mesh):
    rows = P("dp", "graph", None)
    placed = (rows, rows) + (P(),) * 12 + (rows, rows)
    placed += (P("graph", None, None), P("graph"), P("graph"), P("graph"))
    return jax.shard_map(
        shards,
        mesh=mesh,
        in_specs=placed,
        out_specs=(rows,) * 4 + (P(),) * 12,
        check_vma=False,
    )
```

```python
import functools

import jax
import jax.numpy as jnp
from jax import lax
from jax.experimental import pallas as pl
from jax.experimental.pallas import tpu as pltpu
from jax.sharding import PartitionSpec as P

EPS = 1e-05
VMEM = 60 * 1024 * 1024
BLOCK = 16
BATCH = 128
F32 = jnp.float32
BF16 = jnp.bfloat16


def dot(left, right):
    return jnp.dot(left, right, preferred_element_type=F32)


def dot_rows(left, right):
    return lax.dot_general(left, right, (((0,), (0,)), ((), ())), preferred_element_type=F32)


def dot_columns(left, right):
    return lax.dot_general(left, right, (((1,), (1,)), ((), ())), preferred_element_type=F32)


def fold(values):
    rows, width = values.shape
    return jnp.sum(values.reshape(rows // 8, 8, width), axis=0)


def logistic(values):
    return 0.5 * jnp.tanh(0.5 * values) + 0.5


def normalize(values):
    average = jnp.mean(values, axis=-1, keepdims=True)
    centred = values - average
    inverse = lax.rsqrt(jnp.mean(centred * centred, axis=-1, keepdims=True) + EPS)
    return centred * inverse, inverse


def norm_back(scaled, normed, inverse):
    average = jnp.mean(scaled, axis=-1, keepdims=True)
    along = jnp.mean(scaled * normed, axis=-1, keepdims=True)
    return inverse * (scaled - average - normed * along)


def lanes(values, width):
    return jnp.concatenate([values] * (width // values.shape[1]), axis=1)


def lane_parts(values):
    width = values.shape[1]
    return sum(values[:, at : at + 128] for at in range(128, width, 128)) + values[:, :128]


def row_sums(parts):
    return jnp.sum(jnp.concatenate(parts), axis=-1, keepdims=True)


def one_hot_columns(index_column, count):
    lanes = lax.broadcasted_iota(jnp.int32, (index_column.shape[0], count), 1).astype(F32)
    return jnp.where(index_column == lanes, 1.0, 0.0).astype(BF16)


def one_hot_rows(index_row, count):
    rows = lax.broadcasted_iota(jnp.int32, (count, index_row.shape[1]), 0).astype(F32)
    return jnp.where(index_row == rows, 1.0, 0.0).astype(BF16)


def edge_start(idx, x, nodes, first, vec, partial, inputs, table):
    tile, sample = pl.program_id(0), pl.program_id(1)
    width = x.shape[2]
    here = nodes.shape[1]

    @pl.when(tile == 0)
    def _():
        table[sample, :here] = (dot(nodes[sample], first[width : 2 * width]) * 0.5).astype(BF16)
        table[sample, here : 2 * here] = (
            (dot(nodes[sample], first[2 * width :]) + vec[0:1]) * 0.5
        ).astype(BF16)
        table[sample, 2 * here :] = first[:width] * 0.5

    @pl.when(sample == 0)
    def _():
        columns = idx[0].T
        inputs[:, :here] = one_hot_columns(columns[:, 0:1], here)
        inputs[:, here : 2 * here] = one_hot_columns(columns[:, 1:2], here)

    inputs[:, 2 * here :] = x[0]
    partial[0] = dot(inputs[...], table[sample]).astype(BF16)


def edge_forward(
    idx, mask, partial, arrived, send, second, vec,
    nodes_hbm, cot_hbm, node_first_hbm, node_second_hbm,
    act, bend, nrm, inv, vec_grad, nodes_out_hbm, base_hbm, gathered_grad_hbm, weight_grad_hbm,
    inputs, picks, table, live, degree, sums, node_inputs, node_actives, pre_grads, hidden_grads,
    projected, ordered, nodes, cot, node_first, node_second,
    nodes_out, base, gathered_grad, weight_grad, arrive, leave,
):
    tile, sample = pl.program_id(0), pl.program_id(1)
    samples, here, width = nodes.shape
    near = arrived.shape[0]
    slots = arrived.shape[1] // samples
    far = near * slots
    rows = partial.shape[1]
    chunk = rows // 4
    begin = (tile == 0) & (sample == 0)
    end = (tile == pl.num_programs(0) - 1) & (sample == samples - 1)
    incoming = [
        pltpu.make_async_copy(source, target, arrive.at[number])
        for number, (source, target) in enumerate(
            [
                (nodes_hbm, nodes),
                (cot_hbm, cot),
                (node_first_hbm, node_first),
                (node_second_hbm, node_second),
            ]
        )
    ]

    @pl.when(begin)
    def _():
        for copy in incoming:
            copy.start()
        foreign = arrived[...].reshape(samples * far, width)
        projected[...] = dot(foreign, send[...]) * 0.5
        sums[...] = jnp.zeros(sums.shape, F32)
        degree[...] = jnp.zeros(degree.shape, F32)
        table[...] = jnp.zeros(table.shape, BF16)
        for s in range(samples):
            for j in range(near):
                row = (j * samples + s) * slots
                ordered[j * slots : (j + 1) * slots] = projected[row : row + slots]
            table[s, :far] = ordered[...].astype(BF16)

    @pl.when(sample == 0)
    def _():
        columns = idx[0].T
        inputs[...] = one_hot_columns(columns[:, 0:1] - here, table.shape[1])
        live[...] = jnp.broadcast_to(columns[:, 2:3], live.shape)
        chosen = one_hot_rows(idx[0, 1:2], here)
        picks[...] = chosen
        counts = jnp.sum(chosen.astype(F32), axis=-1, keepdims=True)
        degree[...] += jnp.broadcast_to(counts, degree.shape)

    picked, pres = {}, {}

    def pick(number):
        at = slice(number * chunk, (number + 1) * chunk)
        picked[number] = dot(inputs[at], table[sample])

    def activate(number):
        for row in range(0, chunk, BLOCK):
            at = slice(number * chunk + row, number * chunk + row + BLOCK)
            value = partial[0, at].astype(F32) + picked[number][row : row + BLOCK]
            bent = jnp.tanh(value)
            twice = bent + 1.0
            silu = value * twice
            act[0, at] = silu.astype(BF16)
            bend[0, at] = (twice + silu * (1.0 - bent)).astype(BF16)
        pres[number] = dot(act[0, number * chunk : (number + 1) * chunk], second[...])

    def finish(number):
        for first_row in range(0, chunk, chunk // 2):
            batch = range(first_row, first_row + chunk // 2, BLOCK)
            values = [pres[number][row : row + BLOCK] + vec[1:2] for row in batch]
            average = row_sums([lane_parts(value) for value in values]) * (1.0 / width)
            centred = [
                value - average[n * BLOCK : (n + 1) * BLOCK] for n, value in enumerate(values)
            ]
            spread = row_sums([lane_parts(value * value) for value in centred]) * (1.0 / width)
            inverse = lax.rsqrt(spread + EPS)
            for n, row in enumerate(batch):
                at = slice(number * chunk + row, number * chunk + row + BLOCK)
                scale = inverse[n * BLOCK : (n + 1) * BLOCK] * live[at]
                nrm[0, at] = (centred[n] * lanes(scale, width)).astype(BF16)
                inv[0, at] = scale

    stages = (pick, activate, finish)
    for turn in range(4 + len(stages) - 1):
        for stage in reversed(range(len(stages))):
            if 0 <= turn - stage < 4:
                stages[stage](turn - stage)
    sums[sample] += dot(picks[...], nrm[0])

    @pl.when(end)
    def _():
        for copy in incoming:
            copy.wait()
        lines = lax.broadcasted_iota(jnp.int32, (here, 1), 0)
        alive = jnp.where(lines.astype(F32) < jnp.sum(mask[...].astype(F32)), 1.0, 0.0)
        shifts = lanes(degree[...], width) * vec[3:4]
        vectors = [jnp.zeros((8, width), F32) for _ in range(4)]
        hidden, pre, back = {}, {}, {}

        def first_layer(s):
            at = slice(s * here, (s + 1) * here)
            node_inputs[at, :width] = nodes[s]
            node_inputs[at, width:] = (sums[s] * vec[2:3] + shifts).astype(BF16)
            hidden[s] = dot(node_inputs[at], node_first[...])

        def second_layer(s):
            for row in range(0, here, BLOCK):
                at = slice(s * here + row, s * here + row + BLOCK)
                value = hidden[s][row : row + BLOCK] + vec[4:5]
                node_actives[at] = (value * logistic(value)).astype(BF16)
            pre[s] = dot(node_actives[s * here : (s + 1) * here], node_second[...])

        def norm(s):
            for row in range(0, here, BLOCK):
                inside = slice(row, row + BLOCK)
                normed, inverse = normalize(pre[s][inside] + vec[5:6])
                update = alive[inside] * (normed * vec[6:7] + vec[7:8])
                nodes_out[s, inside] = (nodes[s, inside].astype(F32) + update).astype(BF16)
                out_grad = alive[inside] * cot[s, inside].astype(F32)
                vectors[2] += fold(out_grad * normed)
                vectors[3] += fold(out_grad)
                pre_grad = norm_back(out_grad * vec[6:7], normed, inverse)
                vectors[1] += fold(pre_grad)
                pre_grads[s * here + row : s * here + row + BLOCK] = pre_grad.astype(BF16)
            pltpu.make_async_copy(nodes_out.at[s], nodes_out_hbm.at[s], leave.at[s]).start()
            back[s] = dot_columns(pre_grads[s * here : (s + 1) * here], node_second[...])

        def first_back(s):
            for row in range(0, here, BLOCK):
                at = slice(s * here + row, s * here + row + BLOCK)
                value = hidden[s][row : row + BLOCK] + vec[4:5]
                sigma = logistic(value)
                hidden_grad = back[s][row : row + BLOCK] * (sigma + value * sigma * (1.0 - sigma))
                vectors[0] += fold(hidden_grad)
                hidden_grads[at] = hidden_grad.astype(BF16)
            down = dot_columns(hidden_grads[s * here : (s + 1) * here], node_first[...])
            base[s] = cot[s].astype(F32) + down[:, :width]
            gathered_grad[s] = down[:, width:].astype(BF16)
            for number, (source, target) in enumerate(
                [(gathered_grad, gathered_grad_hbm), (base, base_hbm)]
            ):
                pltpu.make_async_copy(
                    source.at[s], target.at[s], leave.at[samples * (1 + number) + s]
                ).start()

        steps = (first_layer, second_layer, norm, first_back)
        for turn in range(samples + len(steps) - 1):
            for stage in reversed(range(len(steps))):
                if 0 <= turn - stage < samples:
                    steps[stage](turn - stage)
        weight_grad[: 2 * width] = dot_rows(node_inputs[...], hidden_grads[...]).astype(BF16)
        weight_grad[2 * width :] = dot_rows(node_actives[...], pre_grads[...]).astype(BF16)
        weights = pltpu.make_async_copy(weight_grad, weight_grad_hbm, leave.at[3 * samples])
        weights.start()
        for number in range(4):
            vec_grad[number] = vectors[number]
        for number, (source, target) in enumerate(
            [(nodes_out, nodes_out_hbm), (gathered_grad, gathered_grad_hbm), (base, base_hbm)]
        ):
            for s in range(samples):
                pltpu.make_async_copy(
                    source.at[s], target.at[s], leave.at[samples * number + s]
                ).wait()
        weights.wait()


def edge_backward(
    idx, early, late, cot, act, late_act, bend, nrm, inv, up, second, vec,
    x_hbm, act_hbm, send_hbm,
    hidden_out, vec_grad, local_hbm, remote_hbm, received_hbm, outbound_hbm, weight_grad_hbm,
    picks, narrow_picks, spread_a, spread_b, turned, pre_a, pre_b, hid_a, hid_b, dead_rows, flags,
    second_t, sums, first_grad, second_grad, ordered,
    final, final_act, send, local, remote, received, outbound, weight_grad, arrive, leave,
):
    step = pl.program_id(0)
    last = pl.num_programs(0) - 1
    samples, here, width = local.shape
    near = outbound.shape[0]
    slots = outbound.shape[1] // samples
    far = near * slots
    senders = here + far
    rows = early.shape[1]
    edges = x_hbm.shape[1]
    pairs = samples // 2
    window = narrow_picks.shape[1]
    pair = step % pairs
    before = 2 * (jnp.maximum(step - 1, 0) % pairs) + 1
    incoming = [
        pltpu.make_async_copy(source, target, arrive.at[number])
        for number, (source, target) in enumerate(
            [
                (x_hbm.at[samples - 1, pl.ds(edges - rows, rows)], final),
                (act_hbm.at[samples - 1, pl.ds(edges - rows, rows)], final_act),
                (send_hbm.at[pl.ds(width, width)], send),
            ]
        )
    ]

    @pl.when(step == 0)
    def _():
        for copy in incoming:
            copy.start()
        first_grad[...] = jnp.zeros(first_grad.shape, F32)
        second_grad[...] = jnp.zeros(second_grad.shape, F32)
        vec_grad[...] = jnp.zeros(vec_grad.shape, F32)
        sums[...] = jnp.zeros(sums.shape, F32)
        turned[width:] = jnp.ones((BLOCK, rows), BF16)
        pre_b[...] = jnp.zeros(pre_b.shape, BF16)
        hid_b[...] = jnp.zeros(hid_b.shape, BF16)
        spread_b[...] = jnp.zeros(spread_b.shape, BF16)
        second_t[...] = (second[...] * 0.5).T

    @pl.when(pair == 0)
    def _():
        receivers = idx[0, 1:2]
        lowest = jnp.min(jnp.where(receivers < 0.0, float(here), receivers)).astype(jnp.int32)
        highest = jnp.max(receivers).astype(jnp.int32)
        start = jnp.minimum(lowest // 16 * 16, here - window)
        flags[0] = (jnp.min(idx[0, 2:3]) < 0.5).astype(jnp.int32)
        flags[1] = (highest < start + window).astype(jnp.int32)
        flags[2] = start
        columns = idx[0].T[:, 1:2]
        picks[...] = one_hot_columns(columns, here)
        narrow_picks[...] = one_hot_columns(columns - start.astype(F32), window)
        dead_rows[...] = jnp.broadcast_to(1.0 - idx[0, 2:3], dead_rows.shape).astype(BF16)
        spread_a[:senders] = one_hot_rows(idx[0, 0:1], senders)
        spread_a[senders:] = one_hot_rows(idx[0, 1:2], here)

    @pl.when(pair == 1)
    def _():
        spread_b[...] = spread_a[...]

    def outer(act, pre):
        def piece(columns):
            if columns.start == 0:
                turned[:width] = act.T
            second_grad[:, columns] += dot(turned[...], pre[:, columns])

        return [lambda at=at: piece(at) for at in sides]

    def input_outer(x, hid):
        transposed = {}

        def piece(columns):
            if not transposed:
                transposed[0] = x.T
            first_grad[:, columns] += dot(transposed[0], hid[:, columns])

        return [lambda at=at: piece(at) for at in sides]

    def scatter(spread, hid, where):
        def piece(columns):
            sums[where, :, columns] += dot(spread[...], hid[:, columns])

        return [lambda at=at: piece(at) for at in sides]

    sides = [slice(0, width // 2), slice(width // 2, width)]

    def main(narrow):
        sums_at = [jnp.zeros((8, width), F32) for _ in range(2)]
        results = {}

        def norm_part(side, pre, first_row):
            batch = range(first_row, first_row + BATCH, BLOCK)
            kept, averages, slopes = [], [], []
            for row in batch:
                at = slice(row, row + BLOCK)
                normed = nrm[side, at].astype(F32)
                scaled = (cot[side, at].astype(F32) + results[side][at]) * vec[2:3]
                along = scaled * normed
                sums_at[0] += fold(along)
                sums_at[1] += fold(scaled)
                kept.append(scaled)
                averages.append(lane_parts(scaled))
                slopes.append(lane_parts(along))
            average = row_sums(averages) * (1.0 / width)
            slope = row_sums(slopes) * (1.0 / width)
            for n, row in enumerate(batch):
                at = slice(row, row + BLOCK)
                inside = slice(n * BLOCK, (n + 1) * BLOCK)
                change = kept[n] - average[inside] - slope[inside] * nrm[side, at].astype(F32)
                pre[at] = (change * lanes(inv[side, at], width)).astype(BF16)

        def silu_part(side, hid, first_row):
            for row in range(first_row, first_row + BATCH, BLOCK):
                at = slice(row, row + BLOCK)
                hidden_grad = (results[2 + side][at] * bend[side, at].astype(F32)).astype(BF16)
                hid[at] = hidden_grad
                hidden_out[side, at] = hidden_grad

        def interleave(part, pieces):
            batches = range(0, rows, BATCH)
            spots = [len(batches) * n // len(pieces) for n in range(len(pieces))]
            for number, row in enumerate(batches):
                while spots and number == spots[0]:
                    spots.pop(0)
                    pieces.pop(0)()
                part(row)

        def pick(side):
            if narrow:
                some = up[side, pl.ds(pl.multiple_of(flags[2], 16), window)]
                results[side] = dot(narrow_picks[...], some)
            else:
                results[side] = dot(picks[...], up[side])

        def back(side, pre):
            results[2 + side] = dot(pre[...], second_t[...])

        pick(0)
        interleave(
            lambda row: norm_part(0, pre_a, row),
            [lambda: pick(1)] + outer(late_act[0], pre_b),
        )
        interleave(
            lambda row: norm_part(1, pre_b, row),
            [lambda: back(0, pre_a)] + input_outer(late[0], hid_b),
        )
        interleave(
            lambda row: silu_part(0, hid_a, row),
            [lambda: back(1, pre_b)] + scatter(spread_b, hid_b, before),
        )
        interleave(
            lambda row: silu_part(1, hid_b, row),
            outer(act[0], pre_a)
            + input_outer(early[0], hid_a)
            + scatter(spread_a, hid_a, 2 * pair),
        )
        for number in range(2):
            vec_grad[2 + number] += sums_at[number]

    @pl.when(flags[1] == 1)
    def _():
        main(True)

    @pl.when(flags[1] == 0)
    def _():
        main(False)

    @pl.when(flags[0] == 1)
    def _():
        extra = dot(dead_rows[...], cot[0]) + dot(dead_rows[...], cot[1])
        vec_grad[3] -= extra[:8] * 0.125 * vec[2:3]

    @pl.when(step == last)
    def _():
        leaving = []

        def send_off(source, target):
            copy = pltpu.make_async_copy(source, target, leave.at[len(leaving)])
            copy.start()
            leaving.append(copy)

        def part(number):
            return pl.ds(number * width, width)

        for copy in incoming:
            copy.wait()
        for piece in outer(final_act[...], pre_b):
            piece()
        weight_grad[3 * width :] = second_grad[:width].astype(BF16)
        vec_grad[1] = second_grad[width : width + 8] * 0.125
        send_off(weight_grad.at[part(3)], weight_grad_hbm.at[part(3)])
        for piece in input_outer(final[...], hid_b) + scatter(spread_b, hid_b, samples - 1):
            piece()
        weight_grad[:width] = first_grad[...].astype(BF16)
        send_off(weight_grad.at[part(0)], weight_grad_hbm.at[part(0)])
        for s in range(samples):
            for j in range(near):
                row, place = here + j * slots, (j * samples + s) * slots
                ordered[place : place + slots] = sums[s, row : row + slots]
        remote[...] = ordered[...].astype(BF16)
        outbound[...] = dot_columns(remote[...], send[...]).astype(BF16).reshape(outbound.shape)
        send_off(outbound, outbound_hbm)
        send_off(remote, remote_hbm)
        local[...] = sums[:, :here].astype(BF16)
        send_off(local, local_hbm)
        received[...] = sums[:, senders:].astype(BF16)
        send_off(received, received_hbm)
        every = jnp.zeros((8, width), F32)
        for s in range(samples):
            every += fold(sums[s, :senders])
        vec_grad[0] = every
        for number in (2, 3):
            vec_grad[number] = vec_grad[number] / vec[2:3]
        for copy in leaving:
            copy.wait()


def edge_totals(
    local, received, remote, nodes, arrived, base, first, weights_in, after,
    node_grad, weights, made, leave,
):
    samples, here, width = nodes.shape
    owned = nodes[...].reshape(samples * here, width)
    mine = local[...].reshape(samples * here, width)
    got = received[...].reshape(samples * here, width)
    foreign = arrived[...].reshape(remote.shape)
    made[:width] = (dot_rows(owned, mine) + dot_rows(foreign, remote[...])).astype(BF16)
    made[width:] = dot_rows(owned, got).astype(BF16)
    copy = pltpu.make_async_copy(made, weights.at[pl.ds(width, 2 * width)], leave)
    copy.start()
    grads = dot_columns(mine, first[width : 2 * width]) + dot_columns(got, first[2 * width :])
    node_grad[...] = base[...] + grads.reshape(node_grad.shape)
    copy.wait()


def edge_outputs(idx, x_low, x_high, nrm_low, nrm_high, vec, after, edges_out, live):
    @pl.when(pl.program_id(1) == 0)
    def _():
        live[...] = jnp.broadcast_to(idx[0].T[:, 2:3], live.shape)

    rows = x_low.shape[1]
    for start, x, nrm in ((0, x_low, nrm_low), (rows, x_high, nrm_high)):
        for row in range(0, rows, BLOCK):
            inside = slice(row, row + BLOCK)
            at = slice(start + row, start + row + BLOCK)
            message = nrm[0, inside].astype(F32) * vec[2:3] + vec[3:4]
            message = jnp.where(lanes(live[at], message.shape[1]) > 0.0, message, 0.0)
            edges_out[0, at] = (x[0, inside].astype(F32) + message).astype(BF16)


def edge_gradient(cot_low, cot_high, hid_low, hid_high, first, after, edge_grad, first_t):
    @pl.when((pl.program_id(0) == 0) & (pl.program_id(1) == 0))
    def _():
        first_t[...] = first[...].T

    rows = cot_low.shape[1]
    for start, cot, hid in ((0, cot_low, hid_low), (rows, cot_high, hid_high)):
        at = slice(start, start + rows)
        edge_grad[0, at] = (cot[0].astype(F32) + dot(hid[0], first_t[...])).astype(BF16)


def unpack(totals, *refs):
    outs, (given, leave) = refs[:-2], refs[-2:]
    rows = given.shape[1]
    width = totals.shape[2]
    edge_half, node_half = 2 * width, (totals.shape[1] - 2 * width) // rows * rows
    places = []
    for core in range(2):
        for start, count, pair in ((0, edge_half, outs[:2]), (edge_half, node_half, outs[2:])):
            for row in range(0, count, rows):
                goal = core * count + row
                if goal < pair[0].shape[0]:
                    places.append((core, start + row, pair[0], goal))
                else:
                    places.append((core, start + row, pair[1], goal - pair[0].shape[0]))
    leaving = []
    for n, (core, row, target, goal) in enumerate(places):
        given[n] = totals[core, row : row + rows].astype(F32)
        copy = pltpu.make_async_copy(given.at[n], target.at[pl.ds(goal, rows)], leave.at[n])
        copy.start()
        leaving.append(copy)
    for copy in leaving:
        copy.wait()


def whole(shape):
    return pl.BlockSpec(
        shape, lambda *_: (0,) * len(shape), pipeline_mode=pl.Buffered(buffer_count=1)
    )


def unread():
    return pl.BlockSpec(memory_space=pl.ANY)


def params(steps):
    return pltpu.CompilerParams(
        dimension_semantics=("arbitrary",) * steps, vmem_limit_bytes=VMEM
    )


def peer_offset(number, near):
    half = near // 2
    return number - half if number < half else number - half + 1


def shift(block, distance):
    size = lax.axis_size("graph")
    return lax.ppermute(block, "graph", [(i, (i + distance) % size) for i in range(size)])


def all_peers(near):
    return lax.axis_size("graph") == near


def exchange(chunks, sign):
    near = chunks.shape[0]
    if not all_peers(near):
        return jnp.stack([shift(chunks[j], sign * peer_offset(j, near)) for j in range(near)])
    me = lax.axis_index("graph")
    swapped = lax.all_to_all(chunks, "graph", 0, 0)
    own = lax.dynamic_index_in_dim(chunks, me, 0, keepdims=False)
    opposite = shift(own, near // 2)
    mine = (jnp.arange(near) == me)[:, None, None]
    return jnp.where(mine, opposite[None], swapped)


def chunk_order(send_index):
    near = send_index.shape[0]
    if not all_peers(near):
        return send_index
    numbers = jnp.arange(near, dtype=jnp.int32)
    distance = (numbers - lax.axis_index("graph") + near) % near
    number = jnp.where(distance <= near // 2, distance + near // 2 - 1, distance - near // 2)
    number = jnp.where(distance == 0, 0, number)
    chosen = number[:, None, None] == numbers[None, :, None]
    return jnp.sum(jnp.where(chosen, send_index[None], 0), axis=1)


def chunk_rows(edge_sender, here, near, slots):
    if not all_peers(near):
        return edge_sender
    slot = edge_sender - here
    number = slot // slots
    offset = number - near // 2 + (number >= near // 2).astype(jnp.int32)
    offset = jnp.where(number == 0, 0, offset)
    owner = (lax.axis_index("graph") - offset + near) % near
    return jnp.where(slot < 0, edge_sender, here + owner * slots + slot % slots)


def rounded(values):
    return lax.reduce_precision(values, 8, 7)


def split_rows(vectors):
    high = rounded(vectors)
    return jnp.concatenate([high, rounded(vectors - high)])


def repeat(block, count):
    return jnp.broadcast_to(block[None], (count,) + block.shape)


def scatter_all(grads):
    rows, width = grads.shape
    parts = 2 * lax.axis_size("graph")
    return lax.all_to_all(grads.reshape(parts, rows // parts, width), ("dp", "graph"), 0, 0)


def add_parts(parts):
    return jnp.sum(parts.astype(F32), axis=0)


def side_groups():
    size = lax.axis_size("graph")
    return [list(range(size // 2)), list(range(size // 2, size))]


def swap_sides(block):
    return shift(block, lax.axis_size("graph") // 2)


def both_sides(piece, other):
    size = lax.axis_size("graph")
    low = lax.axis_index("graph") < size // 2
    return jnp.concatenate([jnp.where(low, piece, other), jnp.where(low, other, piece)])


def exchange_in_side(pieces):
    return lax.all_to_all(pieces, "graph", 0, 0, axis_index_groups=side_groups())


def gather_cores(block):
    return lax.all_to_all(repeat(block, 2), "dp", 0, 0)


def pair_pieces(grads, vectors):
    rows, width = grads.shape
    size = lax.axis_size("graph") // 2
    half = rows // 2
    core = lax.axis_index("dp")
    leaving = lax.dynamic_slice_in_dim(grads, (1 - core) * half, half)
    other = lax.ppermute(leaving, "dp", [(0, 1), (1, 0)])
    mine = lax.dynamic_slice_in_dim(grads, core * half, half)
    pieces = (mine.astype(F32) + other.astype(F32)).astype(BF16)
    pieces = pieces.reshape(size, half // size, width)
    return jnp.concatenate([pieces, repeat(split_rows(vectors).astype(BF16), size)], axis=1)


def shards(
    node_latents,
    edge_latents,
    edge_first,
    edge_first_bias,
    edge_second,
    edge_second_bias,
    edge_gain,
    edge_shift,
    node_first,
    node_first_bias,
    node_second,
    node_second_bias,
    node_gain,
    node_shift,
    node_cot,
    edge_cot,
    send_index,
    edge_sender,
    edge_receiver,
    node_mask,
):
    samples, here, width = node_latents.shape
    edges = edge_latents.shape[1]
    near, slots = send_index.shape[1:]
    far = near * slots
    senders = here + far

    targets = chunk_order(send_index[0])
    targets = targets[:, None, :] + here * jnp.arange(samples, dtype=jnp.int32)[None, :, None]
    pick = jax.nn.one_hot(targets.reshape(-1), samples * here, dtype=BF16)
    parcels = dot(pick, node_latents.reshape(samples * here, width)).astype(BF16)
    arrived = exchange(parcels.reshape(near, samples * slots, width), 1)

    edge_live = edge_receiver < here - 1
    idx = jnp.stack(
        [
            chunk_rows(edge_sender, here, near, slots).astype(F32),
            jnp.where(edge_live, edge_receiver, -1).astype(F32),
            edge_live.astype(F32),
        ]
    )
    idx = jnp.pad(idx, ((0, 5), (0, 0)))
    vec = jnp.stack(
        [edge_first_bias, edge_second_bias, edge_gain, edge_shift]
        + [node_first_bias, node_second_bias, node_gain, node_shift]
    )
    unit = 2 * samples * edges * width * width

    def third(number):
        return pl.BlockSpec(
            (width, width), lambda *_: (number, 0), pipeline_mode=pl.Buffered(buffer_count=1)
        )

    edge_shape = jax.ShapeDtypeStruct((samples, edges, width), BF16)
    inv_shape = jax.ShapeDtypeStruct((samples, edges, 128), F32)
    node_shape = jax.ShapeDtypeStruct((samples, here, width), BF16)
    node_sums_shape = jax.ShapeDtypeStruct((samples, here, width), F32)
    vec_shape = jax.ShapeDtypeStruct((4, 8, width), F32)

    def edge_block(rows):
        return pl.BlockSpec((1, rows, width), lambda t, s: (s, t, 0))

    def two_halves(rows):
        return [
            pl.BlockSpec((1, rows // 2, width), lambda t, s, n=n: (s, 2 * t + n, 0))
            for n in range(2)
        ]

    def idx_block(rows):
        return pl.BlockSpec((1, 8, rows), lambda t, s: (t, 0, 0))

    def inv_block(rows):
        return pl.BlockSpec((1, rows, 128), lambda t, s: (s, t, 0))

    def tiled(rows):
        return idx.reshape(8, edges // rows, rows).transpose(1, 0, 2)

    wide = edges // 2
    partial = pl.pallas_call(
        edge_start,
        grid=(edges // wide, samples),
        in_specs=[
            idx_block(wide),
            edge_block(wide),
            whole((samples, here, width)),
            whole((3 * width, width)),
            whole((8, width)),
        ],
        out_specs=edge_block(wide),
        out_shape=edge_shape,
        scratch_shapes=[
            pltpu.VMEM((wide, 2 * here + width), BF16),
            pltpu.VMEM((samples, 2 * here + width, width), BF16),
        ],
        compiler_params=params(2),
        cost_estimate=pl.CostEstimate(
            flops=3 * unit, bytes_accessed=4 * samples * edges * width, transcendentals=0
        ),
        name="edge_start",
    )(tiled(wide), edge_latents, node_latents, edge_first, vec)

    remote = -(-far // 128) * 128
    (
        act, bend, nrm, inv, node_sums, nodes_out, base, gathered_grad, node_weights
    ) = pl.pallas_call(
        edge_forward,
        grid=(edges // wide, samples),
        in_specs=[
            idx_block(wide),
            whole((1, here)),
            edge_block(wide),
            whole((near, samples * slots, width)),
            third(1),
            whole((width, width)),
            whole((8, width)),
        ]
        + [unread()] * 4,
        out_specs=[edge_block(wide)] * 3
        + [inv_block(wide), whole((4, 8, width))]
        + [unread()] * 4,
        out_shape=[
            edge_shape,
            edge_shape,
            edge_shape,
            inv_shape,
            vec_shape,
            node_shape,
            node_sums_shape,
            node_shape,
            jax.ShapeDtypeStruct((3 * width, width), BF16),
        ],
        scratch_shapes=[
            pltpu.VMEM((wide, remote), BF16),
            pltpu.VMEM((here, wide), BF16),
            pltpu.VMEM((samples, remote, width), BF16),
            pltpu.VMEM((wide, 128), F32),
            pltpu.VMEM((here, 128), F32),
            pltpu.VMEM((samples, here, width), F32),
            pltpu.VMEM((samples * here, 2 * width), BF16),
            pltpu.VMEM((samples * here, width), BF16),
            pltpu.VMEM((samples * here, width), BF16),
            pltpu.VMEM((samples * here, width), BF16),
            pltpu.VMEM((samples * far, width), F32),
            pltpu.VMEM((far, width), F32),
            pltpu.VMEM((samples, here, width), BF16),
            pltpu.VMEM((samples, here, width), BF16),
            pltpu.VMEM((2 * width, width), BF16),
            pltpu.VMEM((width, width), BF16),
            pltpu.VMEM((samples, here, width), BF16),
            pltpu.VMEM((samples, here, width), F32),
            pltpu.VMEM((samples, here, width), BF16),
            pltpu.VMEM((3 * width, width), BF16),
            pltpu.SemaphoreType.DMA((4,)),
            pltpu.SemaphoreType.DMA((3 * samples + 1,)),
        ],
        compiler_params=params(2),
        cost_estimate=pl.CostEstimate(
            flops=4 * unit, bytes_accessed=8 * samples * edges * width, transcendentals=0
        ),
        name="edge_forward",
    )(
        tiled(wide), node_mask[None], partial, arrived, edge_first, edge_second, vec,
        node_latents, node_cot, node_first, node_second,
    )
    node_parts = scatter_all(node_weights)

    short = edges // 5
    pairs = samples // 2

    def paired(lanes_here):
        return pl.BlockSpec((2, short, lanes_here), lambda i: (i % pairs, i // pairs, 0))

    def early_half(i):
        return (2 * (i % pairs), i // pairs, 0)

    def late_half(i):
        j = jnp.maximum(i - 1, 0)
        return (2 * (j % pairs) + 1, j // pairs, 0)

    (
        hidden_grad, edge_sums, local, remote_sums, received, outbound, edge_weights
    ) = pl.pallas_call(
        edge_backward,
        grid=(edges // short * pairs,),
        in_specs=[
            pl.BlockSpec((1, 8, short), lambda i: (i // pairs, 0, 0)),
            pl.BlockSpec((1, short, width), early_half),
            pl.BlockSpec((1, short, width), late_half),
            paired(width),
            pl.BlockSpec((1, short, width), early_half),
            pl.BlockSpec((1, short, width), late_half),
            paired(width),
            paired(width),
            paired(128),
            pl.BlockSpec((2, here, width), lambda i: (i % pairs, 0, 0)),
            whole((width, width)),
            whole((8, width)),
        ]
        + [unread()] * 3,
        out_specs=[paired(width), whole((4, 8, width))] + [unread()] * 5,
        out_shape=[
            edge_shape,
            vec_shape,
            node_shape,
            jax.ShapeDtypeStruct((samples * far, width), BF16),
            node_shape,
            jax.ShapeDtypeStruct((near, samples * slots, width), BF16),
            jax.ShapeDtypeStruct((4 * width, width), BF16),
        ],
        scratch_shapes=[
            pltpu.VMEM((short, here), BF16),
            pltpu.VMEM((short, min(256, here)), BF16),
            pltpu.VMEM((senders + here, short), BF16),
            pltpu.VMEM((senders + here, short), BF16),
            pltpu.VMEM((width + BLOCK, short), BF16),
            pltpu.VMEM((short, width), BF16),
            pltpu.VMEM((short, width), BF16),
            pltpu.VMEM((short, width), BF16),
            pltpu.VMEM((short, width), BF16),
            pltpu.VMEM((BLOCK, short), BF16),
            pltpu.SMEM((3,), jnp.int32),
            pltpu.VMEM((width, width), BF16),
            pltpu.VMEM((samples, senders + here, width), F32),
            pltpu.VMEM((width, width), F32),
            pltpu.VMEM((width + BLOCK, width), F32),
            pltpu.VMEM((samples * far, width), F32),
            pltpu.VMEM((short, width), BF16),
            pltpu.VMEM((short, width), BF16),
            pltpu.VMEM((width, width), BF16),
            pltpu.VMEM((samples, here, width), BF16),
            pltpu.VMEM((samples * far, width), BF16),
            pltpu.VMEM((samples, here, width), BF16),
            pltpu.VMEM((near, samples * slots, width), BF16),
            pltpu.VMEM((4 * width, width), BF16),
            pltpu.SemaphoreType.DMA((3,)),
            pltpu.SemaphoreType.DMA((6,)),
        ],
        compiler_params=params(1),
        cost_estimate=pl.CostEstimate(
            flops=7 * unit, bytes_accessed=10 * samples * edges * width, transcendentals=0
        ),
        name="edge_backward",
    )(
        tiled(short), edge_latents, edge_latents, edge_cot, act, act, bend, nrm, inv,
        gathered_grad, edge_second, vec,
        edge_latents, act, edge_first,
    )
    node_parts, edge_weights, outbound = lax.optimization_barrier(
        (node_parts, edge_weights, outbound)
    )
    returned = exchange(outbound, -1)
    node_partial, edge_weights = pl.pallas_call(
        edge_totals,
        in_specs=[
            whole((samples, here, width)),
            whole((samples, here, width)),
            whole((samples * far, width)),
            whole((samples, here, width)),
            whole((near, samples * slots, width)),
            whole((samples, here, width)),
            whole((3 * width, width)),
            unread(),
            unread(),
        ],
        out_specs=[whole((samples, here, width)), unread()],
        out_shape=[node_sums_shape, jax.ShapeDtypeStruct((4 * width, width), BF16)],
        input_output_aliases={7: 1},
        scratch_shapes=[pltpu.VMEM((2 * width, width), BF16), pltpu.SemaphoreType.DMA],
        compiler_params=pltpu.CompilerParams(vmem_limit_bytes=VMEM),
        name="edge_totals",
    )(
        local, received, remote_sums, node_latents, arrived, base, edge_first, edge_weights,
        outbound,
    )
    vectors = jnp.concatenate([edge_sums, node_sums]).sum(axis=1)
    count = vectors.shape[0]
    pieces = pair_pieces(edge_weights, vectors)
    node_piece = add_parts(node_parts).astype(BF16)
    pieces, returned, node_piece = lax.optimization_barrier((pieces, returned, node_piece))
    arrived_pieces = exchange_in_side(pieces)
    edge_grad = pl.pallas_call(
        edge_gradient,
        grid=(edges // wide, samples),
        in_specs=[*two_halves(wide), *two_halves(wide), third(0), unread()],
        out_specs=edge_block(wide),
        out_shape=edge_shape,
        scratch_shapes=[pltpu.VMEM((width, width), BF16)],
        compiler_params=params(2),
        cost_estimate=pl.CostEstimate(
            flops=unit, bytes_accessed=6 * samples * edges * width, transcendentals=0
        ),
        name="edge_gradient",
    )(edge_cot, edge_cot, hidden_grad, hidden_grad, edge_first, pieces)
    arrived_pieces, edge_grad = lax.optimization_barrier((arrived_pieces, edge_grad))
    partial_sums = add_parts(arrived_pieces)
    piece = partial_sums.shape[0] - 2 * count
    vectors = split_rows(partial_sums[piece : piece + count] + partial_sums[piece + count :])
    partial_sums = jnp.concatenate([rounded(partial_sums[:piece]), vectors])
    other = swap_sides(jnp.concatenate([partial_sums.astype(BF16), node_piece]))
    totals = partial_sums + other[: piece + 2 * count].astype(F32)
    node_pair = both_sides(node_piece, other[piece + 2 * count :])
    vectors = totals[piece : piece + count] + totals[piece + count :]
    joined = jnp.concatenate([totals[:piece].astype(BF16), node_pair])
    gathered_rows = exchange_in_side(repeat(joined, lax.axis_size("graph") // 2))
    edges_out = pl.pallas_call(
        edge_outputs,
        grid=(edges // wide, samples),
        in_specs=[
            idx_block(wide),
            *two_halves(wide),
            *two_halves(wide),
            whole((8, width)),
            unread(),
        ],
        out_specs=edge_block(wide),
        out_shape=edge_shape,
        scratch_shapes=[pltpu.VMEM((wide, 128), F32)],
        compiler_params=params(2),
        cost_estimate=pl.CostEstimate(
            flops=0, bytes_accessed=6 * samples * edges * width, transcendentals=0
        ),
        name="edge_outputs",
    )(
        tiled(wide), edge_latents, edge_latents, nrm, nrm, vec, joined,
    )
    gathered_rows, edges_out = lax.optimization_barrier((gathered_rows, edges_out))
    nodes_rows = gathered_rows[:, piece:]
    nodes_rows = nodes_rows.reshape(nodes_rows.shape[0], 2, -1, width).transpose(1, 0, 2, 3)
    halves = [
        gathered_rows[:, :piece].reshape(2 * width, width),
        nodes_rows.reshape(-1, width),
    ]
    totals = gather_cores(jnp.concatenate(halves + [split_rows(vectors).astype(BF16)]))
    chunk = width // 2
    parts = 7 * width // chunk
    weights = pl.pallas_call(
        unpack,
        in_specs=[pl.BlockSpec(memory_space=pltpu.VMEM)],
        out_specs=[unread()] * 4,
        out_shape=[
            jax.ShapeDtypeStruct((rows * width, width), F32) for rows in (3, 1, 2, 1)
        ],
        scratch_shapes=[
            pltpu.VMEM((parts, chunk, width), F32),
            pltpu.SemaphoreType.DMA((parts,)),
        ],
        compiler_params=pltpu.CompilerParams(vmem_limit_bytes=VMEM),
        name="unpack",
    )(totals)
    vectors = totals[:, -2 * count :].astype(F32).sum(axis=0)
    vectors = vectors[:count] + vectors[count:]

    node_grad = node_partial + dot_rows(pick, returned.reshape(-1, width)).reshape(
        samples, here, width
    )
    return (
        nodes_out,
        edges_out,
        node_grad,
        edge_grad,
        weights[0],
        vectors[0],
        weights[1],
        vectors[1],
        vectors[2],
        vectors[3],
        weights[2],
        vectors[4],
        weights[3],
        vectors[5],
        vectors[6],
        vectors[7],
    )


def solution(mesh):
    rows = P("dp", "graph", None)
    placed = (rows, rows) + (P(),) * 12 + (rows, rows)
    placed += (P("graph", None, None), P("graph"), P("graph"), P("graph"))
    return jax.shard_map(
        shards,
        mesh=mesh,
        in_specs=placed,
        out_specs=(rows,) * 4 + (P(),) * 12,
        check_vma=False,
    )
```

```python
import functools

import jax
import jax.numpy as jnp
from jax import lax
from jax.experimental import pallas as pl
from jax.experimental.pallas import tpu as pltpu
from jax.sharding import PartitionSpec as P

EPS = 1e-05
VMEM = 60 * 1024 * 1024
BLOCK = 16
BATCH = 128
F32 = jnp.float32
BF16 = jnp.bfloat16


def dot(left, right):
    return jnp.dot(left, right, preferred_element_type=F32)


def dot_rows(left, right):
    return lax.dot_general(left, right, (((0,), (0,)), ((), ())), preferred_element_type=F32)


def dot_columns(left, right):
    return lax.dot_general(left, right, (((1,), (1,)), ((), ())), preferred_element_type=F32)


def fold(values):
    rows, width = values.shape
    return jnp.sum(values.reshape(rows // 8, 8, width), axis=0)


def logistic(values):
    return 0.5 * jnp.tanh(0.5 * values) + 0.5


def normalize(values):
    average = jnp.mean(values, axis=-1, keepdims=True)
    centred = values - average
    inverse = lax.rsqrt(jnp.mean(centred * centred, axis=-1, keepdims=True) + EPS)
    return centred * inverse, inverse


def norm_back(scaled, normed, inverse):
    average = jnp.mean(scaled, axis=-1, keepdims=True)
    along = jnp.mean(scaled * normed, axis=-1, keepdims=True)
    return inverse * (scaled - average - normed * along)


def lanes(values, width):
    return jnp.concatenate([values] * (width // values.shape[1]), axis=1)


def lane_parts(values):
    width = values.shape[1]
    return sum(values[:, at : at + 128] for at in range(128, width, 128)) + values[:, :128]


def row_sums(parts):
    return jnp.sum(jnp.concatenate(parts), axis=-1, keepdims=True)


def one_hot_columns(index_column, count):
    lanes = lax.broadcasted_iota(jnp.int32, (index_column.shape[0], count), 1).astype(F32)
    return jnp.where(index_column == lanes, 1.0, 0.0).astype(BF16)


def one_hot_rows(index_row, count):
    rows = lax.broadcasted_iota(jnp.int32, (count, index_row.shape[1]), 0).astype(F32)
    return jnp.where(index_row == rows, 1.0, 0.0).astype(BF16)


def edge_start(idx, x, nodes, first, vec, partial, inputs, table):
    tile, sample = pl.program_id(0), pl.program_id(1)
    width = x.shape[2]
    here = nodes.shape[1]

    @pl.when(tile == 0)
    def _():
        table[sample, :here] = (dot(nodes[sample], first[width : 2 * width]) * 0.5).astype(BF16)
        table[sample, here : 2 * here] = (
            (dot(nodes[sample], first[2 * width :]) + vec[0:1]) * 0.5
        ).astype(BF16)
        table[sample, 2 * here :] = first[:width] * 0.5

    @pl.when(sample == 0)
    def _():
        columns = idx[0].T
        inputs[:, :here] = one_hot_columns(columns[:, 0:1], here)
        inputs[:, here : 2 * here] = one_hot_columns(columns[:, 1:2], here)

    inputs[:, 2 * here :] = x[0]
    partial[0] = dot(inputs[...], table[sample]).astype(BF16)


def edge_forward(
    idx, mask, partial, arrived, send, second, vec,
    nodes_hbm, cot_hbm, node_first_hbm, node_second_hbm,
    act, bend, nrm, inv, vec_grad, nodes_out_hbm, base_hbm, gathered_grad_hbm, weight_grad_hbm,
    inputs, picks, table, live, degree, sums, node_inputs, node_actives, pre_grads, hidden_grads,
    projected, ordered, nodes, cot, node_first, node_second,
    nodes_out, base, gathered_grad, weight_grad, arrive, leave,
):
    tile, sample = pl.program_id(0), pl.program_id(1)
    samples, here, width = nodes.shape
    near = arrived.shape[0]
    slots = arrived.shape[1] // samples
    far = near * slots
    rows = partial.shape[1]
    chunk = rows // 4
    begin = (tile == 0) & (sample == 0)
    end = (tile == pl.num_programs(0) - 1) & (sample == samples - 1)
    incoming = [
        pltpu.make_async_copy(source, target, arrive.at[number])
        for number, (source, target) in enumerate(
            [
                (nodes_hbm, nodes),
                (cot_hbm, cot),
                (node_first_hbm, node_first),
                (node_second_hbm, node_second),
            ]
        )
    ]

    @pl.when(begin)
    def _():
        for copy in incoming:
            copy.start()
        foreign = arrived[...].reshape(samples * far, width)
        projected[...] = dot(foreign, send[...]) * 0.5
        sums[...] = jnp.zeros(sums.shape, F32)
        degree[...] = jnp.zeros(degree.shape, F32)
        table[...] = jnp.zeros(table.shape, BF16)
        for s in range(samples):
            for j in range(near):
                row = (j * samples + s) * slots
                ordered[j * slots : (j + 1) * slots] = projected[row : row + slots]
            table[s, :far] = ordered[...].astype(BF16)

    @pl.when(sample == 0)
    def _():
        columns = idx[0].T
        inputs[...] = one_hot_columns(columns[:, 0:1] - here, table.shape[1])
        live[...] = jnp.broadcast_to(columns[:, 2:3], live.shape)
        chosen = one_hot_rows(idx[0, 1:2], here)
        picks[...] = chosen
        counts = jnp.sum(chosen.astype(F32), axis=-1, keepdims=True)
        degree[...] += jnp.broadcast_to(counts, degree.shape)

    picked, pres = {}, {}

    def pick(number):
        at = slice(number * chunk, (number + 1) * chunk)
        picked[number] = dot(inputs[at], table[sample])

    def activate(number):
        for row in range(0, chunk, BLOCK):
            at = slice(number * chunk + row, number * chunk + row + BLOCK)
            value = partial[0, at].astype(F32) + picked[number][row : row + BLOCK]
            bent = jnp.tanh(value)
            twice = bent + 1.0
            silu = value * twice
            act[0, at] = silu.astype(BF16)
            bend[0, at] = (twice + silu * (1.0 - bent)).astype(BF16)
        pres[number] = dot(act[0, number * chunk : (number + 1) * chunk], second[...])

    def finish(number):
        for first_row in range(0, chunk, chunk // 2):
            batch = range(first_row, first_row + chunk // 2, BLOCK)
            values = [pres[number][row : row + BLOCK] + vec[1:2] for row in batch]
            average = row_sums([lane_parts(value) for value in values]) * (1.0 / width)
            centred = [
                value - average[n * BLOCK : (n + 1) * BLOCK] for n, value in enumerate(values)
            ]
            spread = row_sums([lane_parts(value * value) for value in centred]) * (1.0 / width)
            inverse = lax.rsqrt(spread + EPS)
            for n, row in enumerate(batch):
                at = slice(number * chunk + row, number * chunk + row + BLOCK)
                scale = inverse[n * BLOCK : (n + 1) * BLOCK] * live[at]
                nrm[0, at] = (centred[n] * lanes(scale, width)).astype(BF16)
                inv[0, at] = scale

    stages = (pick, activate, finish)
    for turn in range(4 + len(stages) - 1):
        for stage in reversed(range(len(stages))):
            if 0 <= turn - stage < 4:
                stages[stage](turn - stage)
    sums[sample] += dot(picks[...], nrm[0])

    @pl.when(end)
    def _():
        for copy in incoming:
            copy.wait()
        lines = lax.broadcasted_iota(jnp.int32, (here, 1), 0)
        alive = jnp.where(lines.astype(F32) < jnp.sum(mask[...].astype(F32)), 1.0, 0.0)
        shifts = lanes(degree[...], width) * vec[3:4]
        vectors = [jnp.zeros((8, width), F32) for _ in range(4)]
        hidden, pre, back = {}, {}, {}

        def first_layer(s):
            at = slice(s * here, (s + 1) * here)
            node_inputs[at, :width] = nodes[s]
            node_inputs[at, width:] = (sums[s] * vec[2:3] + shifts).astype(BF16)
            hidden[s] = dot(node_inputs[at], node_first[...])

        def second_layer(s):
            for row in range(0, here, BLOCK):
                at = slice(s * here + row, s * here + row + BLOCK)
                value = hidden[s][row : row + BLOCK] + vec[4:5]
                node_actives[at] = (value * logistic(value)).astype(BF16)
            pre[s] = dot(node_actives[s * here : (s + 1) * here], node_second[...])

        def norm(s):
            for row in range(0, here, BLOCK):
                inside = slice(row, row + BLOCK)
                normed, inverse = normalize(pre[s][inside] + vec[5:6])
                update = alive[inside] * (normed * vec[6:7] + vec[7:8])
                nodes_out[s, inside] = (nodes[s, inside].astype(F32) + update).astype(BF16)
                out_grad = alive[inside] * cot[s, inside].astype(F32)
                vectors[2] += fold(out_grad * normed)
                vectors[3] += fold(out_grad)
                pre_grad = norm_back(out_grad * vec[6:7], normed, inverse)
                vectors[1] += fold(pre_grad)
                pre_grads[s * here + row : s * here + row + BLOCK] = pre_grad.astype(BF16)
            pltpu.make_async_copy(nodes_out.at[s], nodes_out_hbm.at[s], leave.at[s]).start()
            back[s] = dot_columns(pre_grads[s * here : (s + 1) * here], node_second[...])

        def first_back(s):
            for row in range(0, here, BLOCK):
                at = slice(s * here + row, s * here + row + BLOCK)
                value = hidden[s][row : row + BLOCK] + vec[4:5]
                sigma = logistic(value)
                hidden_grad = back[s][row : row + BLOCK] * (sigma + value * sigma * (1.0 - sigma))
                vectors[0] += fold(hidden_grad)
                hidden_grads[at] = hidden_grad.astype(BF16)
            down = dot_columns(hidden_grads[s * here : (s + 1) * here], node_first[...])
            base[s] = cot[s].astype(F32) + down[:, :width]
            gathered_grad[s] = down[:, width:].astype(BF16)
            for number, (source, target) in enumerate(
                [(gathered_grad, gathered_grad_hbm), (base, base_hbm)]
            ):
                pltpu.make_async_copy(
                    source.at[s], target.at[s], leave.at[samples * (1 + number) + s]
                ).start()

        steps = (first_layer, second_layer, norm, first_back)
        for turn in range(samples + len(steps) - 1):
            for stage in reversed(range(len(steps))):
                if 0 <= turn - stage < samples:
                    steps[stage](turn - stage)
        weight_grad[: 2 * width] = dot_rows(node_inputs[...], hidden_grads[...]).astype(BF16)
        weight_grad[2 * width :] = dot_rows(node_actives[...], pre_grads[...]).astype(BF16)
        weights = pltpu.make_async_copy(weight_grad, weight_grad_hbm, leave.at[3 * samples])
        weights.start()
        for number in range(4):
            vec_grad[number] = vectors[number]
        for number, (source, target) in enumerate(
            [(nodes_out, nodes_out_hbm), (gathered_grad, gathered_grad_hbm), (base, base_hbm)]
        ):
            for s in range(samples):
                pltpu.make_async_copy(
                    source.at[s], target.at[s], leave.at[samples * number + s]
                ).wait()
        weights.wait()


def edge_backward(
    idx, early, late, cot, act, late_act, bend, nrm, inv, up, second, vec,
    x_hbm, act_hbm, send_hbm,
    hidden_out, vec_grad, local_hbm, remote_hbm, received_hbm, outbound_hbm, weight_grad_hbm,
    picks, narrow_picks, spread_a, spread_b, turned, pre_a, pre_b, hid_a, hid_b, dead_rows, flags,
    second_t, sums, first_grad, second_grad, ordered,
    final, final_act, send, local, remote, received, outbound, weight_grad, arrive, leave,
):
    step = pl.program_id(0)
    last = pl.num_programs(0) - 1
    samples, here, width = local.shape
    near = outbound.shape[0]
    slots = outbound.shape[1] // samples
    far = near * slots
    senders = here + far
    rows = early.shape[1]
    edges = x_hbm.shape[1]
    pairs = samples // 2
    window = narrow_picks.shape[1]
    pair = step % pairs
    before = 2 * (jnp.maximum(step - 1, 0) % pairs) + 1
    incoming = [
        pltpu.make_async_copy(source, target, arrive.at[number])
        for number, (source, target) in enumerate(
            [
                (x_hbm.at[samples - 1, pl.ds(edges - rows, rows)], final),
                (act_hbm.at[samples - 1, pl.ds(edges - rows, rows)], final_act),
                (send_hbm.at[pl.ds(width, width)], send),
            ]
        )
    ]

    @pl.when(step == 0)
    def _():
        for copy in incoming:
            copy.start()
        first_grad[...] = jnp.zeros(first_grad.shape, F32)
        second_grad[...] = jnp.zeros(second_grad.shape, F32)
        vec_grad[...] = jnp.zeros(vec_grad.shape, F32)
        sums[...] = jnp.zeros(sums.shape, F32)
        turned[width:] = jnp.ones((BLOCK, rows), BF16)
        pre_b[...] = jnp.zeros(pre_b.shape, BF16)
        hid_b[...] = jnp.zeros(hid_b.shape, BF16)
        spread_b[...] = jnp.zeros(spread_b.shape, BF16)
        second_t[...] = (second[...] * 0.5).T

    @pl.when(pair == 0)
    def _():
        receivers = idx[0, 1:2]
        lowest = jnp.min(jnp.where(receivers < 0.0, float(here), receivers)).astype(jnp.int32)
        highest = jnp.max(receivers).astype(jnp.int32)
        start = jnp.minimum(lowest // 16 * 16, here - window)
        flags[0] = (jnp.min(idx[0, 2:3]) < 0.5).astype(jnp.int32)
        flags[1] = (highest < start + window).astype(jnp.int32)
        flags[2] = start
        columns = idx[0].T[:, 1:2]
        picks[...] = one_hot_columns(columns, here)
        narrow_picks[...] = one_hot_columns(columns - start.astype(F32), window)
        dead_rows[...] = jnp.broadcast_to(1.0 - idx[0, 2:3], dead_rows.shape).astype(BF16)
        spread_a[:senders] = one_hot_rows(idx[0, 0:1], senders)
        spread_a[senders:] = one_hot_rows(idx[0, 1:2], here)

    @pl.when(pair == 1)
    def _():
        spread_b[...] = spread_a[...]

    def outer(act, pre):
        def piece(columns):
            if columns.start == 0:
                turned[:width] = act.T
            second_grad[:, columns] += dot(turned[...], pre[:, columns])

        return [lambda at=at: piece(at) for at in sides]

    def input_outer(x, hid):
        transposed = {}

        def piece(columns):
            if not transposed:
                transposed[0] = x.T
            first_grad[:, columns] += dot(transposed[0], hid[:, columns])

        return [lambda at=at: piece(at) for at in sides]

    def scatter(spread, hid, where):
        def piece(columns):
            sums[where, :, columns] += dot(spread[...], hid[:, columns])

        return [lambda at=at: piece(at) for at in sides]

    sides = [slice(0, width // 2), slice(width // 2, width)]

    def main(narrow):
        sums_at = [jnp.zeros((8, width), F32) for _ in range(2)]
        results = {}

        def norm_part(side, pre, first_row):
            batch = range(first_row, first_row + BATCH, BLOCK)
            kept, averages, slopes = [], [], []
            for row in batch:
                at = slice(row, row + BLOCK)
                normed = nrm[side, at].astype(F32)
                scaled = (cot[side, at].astype(F32) + results[side][at]) * vec[2:3]
                along = scaled * normed
                sums_at[0] += fold(along)
                sums_at[1] += fold(scaled)
                kept.append(scaled)
                averages.append(lane_parts(scaled))
                slopes.append(lane_parts(along))
            average = row_sums(averages) * (1.0 / width)
            slope = row_sums(slopes) * (1.0 / width)
            for n, row in enumerate(batch):
                at = slice(row, row + BLOCK)
                inside = slice(n * BLOCK, (n + 1) * BLOCK)
                change = kept[n] - average[inside] - slope[inside] * nrm[side, at].astype(F32)
                pre[at] = (change * lanes(inv[side, at], width)).astype(BF16)

        def silu_part(side, hid, first_row):
            for row in range(first_row, first_row + BATCH, BLOCK):
                at = slice(row, row + BLOCK)
                hidden_grad = (results[2 + side][at] * bend[side, at].astype(F32)).astype(BF16)
                hid[at] = hidden_grad
                hidden_out[side, at] = hidden_grad

        def interleave(part, pieces):
            batches = range(0, rows, BATCH)
            spots = [len(batches) * n // len(pieces) for n in range(len(pieces))]
            for number, row in enumerate(batches):
                while spots and number == spots[0]:
                    spots.pop(0)
                    pieces.pop(0)()
                part(row)

        def pick(side):
            if narrow:
                some = up[side, pl.ds(pl.multiple_of(flags[2], 16), window)]
                results[side] = dot(narrow_picks[...], some)
            else:
                results[side] = dot(picks[...], up[side])

        def back(side, pre):
            results[2 + side] = dot(pre[...], second_t[...])

        pick(0)
        interleave(
            lambda row: norm_part(0, pre_a, row),
            [lambda: pick(1)] + outer(late_act[0], pre_b),
        )
        interleave(
            lambda row: norm_part(1, pre_b, row),
            [lambda: back(0, pre_a)] + input_outer(late[0], hid_b),
        )
        interleave(
            lambda row: silu_part(0, hid_a, row),
            [lambda: back(1, pre_b)] + scatter(spread_b, hid_b, before),
        )
        interleave(
            lambda row: silu_part(1, hid_b, row),
            outer(act[0], pre_a)
            + input_outer(early[0], hid_a)
            + scatter(spread_a, hid_a, 2 * pair),
        )
        for number in range(2):
            vec_grad[2 + number] += sums_at[number]

    @pl.when(flags[1] == 1)
    def _():
        main(True)

    @pl.when(flags[1] == 0)
    def _():
        main(False)

    @pl.when(flags[0] == 1)
    def _():
        extra = dot(dead_rows[...], cot[0]) + dot(dead_rows[...], cot[1])
        vec_grad[3] -= extra[:8] * 0.125 * vec[2:3]

    @pl.when(step == last)
    def _():
        leaving = []

        def send_off(source, target):
            copy = pltpu.make_async_copy(source, target, leave.at[len(leaving)])
            copy.start()
            leaving.append(copy)

        def part(number):
            return pl.ds(number * width, width)

        for copy in incoming:
            copy.wait()
        for piece in outer(final_act[...], pre_b):
            piece()
        weight_grad[3 * width :] = second_grad[:width].astype(BF16)
        vec_grad[1] = second_grad[width : width + 8] * 0.125
        send_off(weight_grad.at[part(3)], weight_grad_hbm.at[part(3)])
        for piece in input_outer(final[...], hid_b) + scatter(spread_b, hid_b, samples - 1):
            piece()
        weight_grad[:width] = first_grad[...].astype(BF16)
        send_off(weight_grad.at[part(0)], weight_grad_hbm.at[part(0)])
        for s in range(samples):
            for j in range(near):
                row, place = here + j * slots, (j * samples + s) * slots
                ordered[place : place + slots] = sums[s, row : row + slots]
        remote[...] = ordered[...].astype(BF16)
        outbound[...] = dot_columns(remote[...], send[...]).astype(BF16).reshape(outbound.shape)
        send_off(outbound, outbound_hbm)
        send_off(remote, remote_hbm)
        local[...] = sums[:, :here].astype(BF16)
        send_off(local, local_hbm)
        received[...] = sums[:, senders:].astype(BF16)
        send_off(received, received_hbm)
        every = jnp.zeros((8, width), F32)
        for s in range(samples):
            every += fold(sums[s, :senders])
        vec_grad[0] = every
        for number in (2, 3):
            vec_grad[number] = vec_grad[number] / vec[2:3]
        for copy in leaving:
            copy.wait()


def edge_totals(
    local, received, remote, nodes, arrived, base, first, weights_in, after,
    node_grad, weights, made, leave,
):
    samples, here, width = nodes.shape
    owned = nodes[...].reshape(samples * here, width)
    mine = local[...].reshape(samples * here, width)
    got = received[...].reshape(samples * here, width)
    foreign = arrived[...].reshape(remote.shape)
    made[:width] = (dot_rows(owned, mine) + dot_rows(foreign, remote[...])).astype(BF16)
    made[width:] = dot_rows(owned, got).astype(BF16)
    copy = pltpu.make_async_copy(made, weights.at[pl.ds(width, 2 * width)], leave)
    copy.start()
    grads = dot_columns(mine, first[width : 2 * width]) + dot_columns(got, first[2 * width :])
    node_grad[...] = base[...] + grads.reshape(node_grad.shape)
    copy.wait()


def edge_outputs(idx, x_low, x_high, nrm_low, nrm_high, vec, after, edges_out, live):
    @pl.when(pl.program_id(1) == 0)
    def _():
        live[...] = jnp.broadcast_to(idx[0].T[:, 2:3], live.shape)

    rows = x_low.shape[1]
    for start, x, nrm in ((0, x_low, nrm_low), (rows, x_high, nrm_high)):
        for row in range(0, rows, BLOCK):
            inside = slice(row, row + BLOCK)
            at = slice(start + row, start + row + BLOCK)
            message = nrm[0, inside].astype(F32) * vec[2:3] + vec[3:4]
            message = jnp.where(lanes(live[at], message.shape[1]) > 0.0, message, 0.0)
            edges_out[0, at] = (x[0, inside].astype(F32) + message).astype(BF16)


def edge_gradient(cot_low, cot_high, hid_low, hid_high, first, after, edge_grad, first_t):
    @pl.when((pl.program_id(0) == 0) & (pl.program_id(1) == 0))
    def _():
        first_t[...] = first[...].T

    rows = cot_low.shape[1]
    for start, cot, hid in ((0, cot_low, hid_low), (rows, cot_high, hid_high)):
        at = slice(start, start + rows)
        edge_grad[0, at] = (cot[0].astype(F32) + dot(hid[0], first_t[...])).astype(BF16)


def unpack(totals, *refs):
    outs, (taken, given, arrive, leave) = refs[:-4], refs[-4:]
    rows = taken.shape[1]
    width = totals.shape[2]
    edge_half, node_half = 2 * width, (totals.shape[1] - 2 * width) // rows * rows
    places = []
    for core in range(2):
        for start, count, pair in ((0, edge_half, outs[:2]), (edge_half, node_half, outs[2:])):
            for row in range(0, count, rows):
                goal = core * count + row
                if goal < pair[0].shape[0]:
                    places.append((core, start + row, pair[0], goal))
                else:
                    places.append((core, start + row, pair[1], goal - pair[0].shape[0]))
    incoming = [
        pltpu.make_async_copy(totals.at[core, pl.ds(row, rows)], taken.at[n], arrive.at[n])
        for n, (core, row, _, _) in enumerate(places)
    ]
    leaving = [
        pltpu.make_async_copy(given.at[n], goal.at[pl.ds(row, rows)], leave.at[n])
        for n, (_, _, goal, row) in enumerate(places)
    ]
    for copy in incoming:
        copy.start()
    for n in range(len(places)):
        incoming[n].wait()
        given[n] = taken[n].astype(F32)
        leaving[n].start()
    for copy in leaving:
        copy.wait()


def whole(shape):
    return pl.BlockSpec(
        shape, lambda *_: (0,) * len(shape), pipeline_mode=pl.Buffered(buffer_count=1)
    )


def unread():
    return pl.BlockSpec(memory_space=pl.ANY)


def params(steps):
    return pltpu.CompilerParams(
        dimension_semantics=("arbitrary",) * steps, vmem_limit_bytes=VMEM
    )


def peer_offset(number, near):
    half = near // 2
    return number - half if number < half else number - half + 1


def shift(block, distance):
    size = lax.axis_size("graph")
    return lax.ppermute(block, "graph", [(i, (i + distance) % size) for i in range(size)])


def all_peers(near):
    return lax.axis_size("graph") == near


def exchange(chunks, sign):
    near = chunks.shape[0]
    if not all_peers(near):
        return jnp.stack([shift(chunks[j], sign * peer_offset(j, near)) for j in range(near)])
    me = lax.axis_index("graph")
    swapped = lax.all_to_all(chunks, "graph", 0, 0)
    own = lax.dynamic_index_in_dim(chunks, me, 0, keepdims=False)
    opposite = shift(own, near // 2)
    mine = (jnp.arange(near) == me)[:, None, None]
    return jnp.where(mine, opposite[None], swapped)


def chunk_order(send_index):
    near = send_index.shape[0]
    if not all_peers(near):
        return send_index
    numbers = jnp.arange(near, dtype=jnp.int32)
    distance = (numbers - lax.axis_index("graph") + near) % near
    number = jnp.where(distance <= near // 2, distance + near // 2 - 1, distance - near // 2)
    number = jnp.where(distance == 0, 0, number)
    chosen = number[:, None, None] == numbers[None, :, None]
    return jnp.sum(jnp.where(chosen, send_index[None], 0), axis=1)


def chunk_rows(edge_sender, here, near, slots):
    if not all_peers(near):
        return edge_sender
    slot = edge_sender - here
    number = slot // slots
    offset = number - near // 2 + (number >= near // 2).astype(jnp.int32)
    offset = jnp.where(number == 0, 0, offset)
    owner = (lax.axis_index("graph") - offset + near) % near
    return jnp.where(slot < 0, edge_sender, here + owner * slots + slot % slots)


def rounded(values):
    return lax.reduce_precision(values, 8, 7)


def split_rows(vectors):
    high = rounded(vectors)
    return jnp.concatenate([high, rounded(vectors - high)])


def repeat(block, count):
    return jnp.broadcast_to(block[None], (count,) + block.shape)


def scatter_all(grads):
    rows, width = grads.shape
    parts = 2 * lax.axis_size("graph")
    return lax.all_to_all(grads.reshape(parts, rows // parts, width), ("dp", "graph"), 0, 0)


def add_parts(parts):
    return jnp.sum(parts.astype(F32), axis=0)


def side_groups():
    size = lax.axis_size("graph")
    return [list(range(size // 2)), list(range(size // 2, size))]


def swap_sides(block):
    return shift(block, lax.axis_size("graph") // 2)


def both_sides(piece, other):
    size = lax.axis_size("graph")
    low = lax.axis_index("graph") < size // 2
    return jnp.concatenate([jnp.where(low, piece, other), jnp.where(low, other, piece)])


def exchange_in_side(pieces):
    return lax.all_to_all(pieces, "graph", 0, 0, axis_index_groups=side_groups())


def gather_cores(block):
    return lax.all_to_all(repeat(block, 2), "dp", 0, 0)


def pair_pieces(grads, vectors):
    rows, width = grads.shape
    size = lax.axis_size("graph") // 2
    half = rows // 2
    core = lax.axis_index("dp")
    leaving = lax.dynamic_slice_in_dim(grads, (1 - core) * half, half)
    other = lax.ppermute(leaving, "dp", [(0, 1), (1, 0)])
    mine = lax.dynamic_slice_in_dim(grads, core * half, half)
    pieces = (mine.astype(F32) + other.astype(F32)).astype(BF16)
    pieces = pieces.reshape(size, half // size, width)
    return jnp.concatenate([pieces, repeat(split_rows(vectors).astype(BF16), size)], axis=1)


def shards(
    node_latents,
    edge_latents,
    edge_first,
    edge_first_bias,
    edge_second,
    edge_second_bias,
    edge_gain,
    edge_shift,
    node_first,
    node_first_bias,
    node_second,
    node_second_bias,
    node_gain,
    node_shift,
    node_cot,
    edge_cot,
    send_index,
    edge_sender,
    edge_receiver,
    node_mask,
):
    samples, here, width = node_latents.shape
    edges = edge_latents.shape[1]
    near, slots = send_index.shape[1:]
    far = near * slots
    senders = here + far

    targets = chunk_order(send_index[0])
    targets = targets[:, None, :] + here * jnp.arange(samples, dtype=jnp.int32)[None, :, None]
    pick = jax.nn.one_hot(targets.reshape(-1), samples * here, dtype=BF16)
    parcels = dot(pick, node_latents.reshape(samples * here, width)).astype(BF16)
    arrived = exchange(parcels.reshape(near, samples * slots, width), 1)

    edge_live = edge_receiver < here - 1
    idx = jnp.stack(
        [
            chunk_rows(edge_sender, here, near, slots).astype(F32),
            jnp.where(edge_live, edge_receiver, -1).astype(F32),
            edge_live.astype(F32),
        ]
    )
    idx = jnp.pad(idx, ((0, 5), (0, 0)))
    vec = jnp.stack(
        [edge_first_bias, edge_second_bias, edge_gain, edge_shift]
        + [node_first_bias, node_second_bias, node_gain, node_shift]
    )
    unit = 2 * samples * edges * width * width

    def third(number):
        return pl.BlockSpec(
            (width, width), lambda *_: (number, 0), pipeline_mode=pl.Buffered(buffer_count=1)
        )

    edge_shape = jax.ShapeDtypeStruct((samples, edges, width), BF16)
    inv_shape = jax.ShapeDtypeStruct((samples, edges, 128), F32)
    node_shape = jax.ShapeDtypeStruct((samples, here, width), BF16)
    node_sums_shape = jax.ShapeDtypeStruct((samples, here, width), F32)
    vec_shape = jax.ShapeDtypeStruct((4, 8, width), F32)

    def edge_block(rows):
        return pl.BlockSpec((1, rows, width), lambda t, s: (s, t, 0))

    def two_halves(rows):
        return [
            pl.BlockSpec((1, rows // 2, width), lambda t, s, n=n: (s, 2 * t + n, 0))
            for n in range(2)
        ]

    def idx_block(rows):
        return pl.BlockSpec((1, 8, rows), lambda t, s: (t, 0, 0))

    def inv_block(rows):
        return pl.BlockSpec((1, rows, 128), lambda t, s: (s, t, 0))

    def tiled(rows):
        return idx.reshape(8, edges // rows, rows).transpose(1, 0, 2)

    wide = edges // 2
    partial = pl.pallas_call(
        edge_start,
        grid=(edges // wide, samples),
        in_specs=[
            idx_block(wide),
            edge_block(wide),
            whole((samples, here, width)),
            whole((3 * width, width)),
            whole((8, width)),
        ],
        out_specs=edge_block(wide),
        out_shape=edge_shape,
        scratch_shapes=[
            pltpu.VMEM((wide, 2 * here + width), BF16),
            pltpu.VMEM((samples, 2 * here + width, width), BF16),
        ],
        compiler_params=params(2),
        cost_estimate=pl.CostEstimate(
            flops=3 * unit, bytes_accessed=4 * samples * edges * width, transcendentals=0
        ),
        name="edge_start",
    )(tiled(wide), edge_latents, node_latents, edge_first, vec)

    remote = -(-far // 128) * 128
    (
        act, bend, nrm, inv, node_sums, nodes_out, base, gathered_grad, node_weights
    ) = pl.pallas_call(
        edge_forward,
        grid=(edges // wide, samples),
        in_specs=[
            idx_block(wide),
            whole((1, here)),
            edge_block(wide),
            whole((near, samples * slots, width)),
            third(1),
            whole((width, width)),
            whole((8, width)),
        ]
        + [unread()] * 4,
        out_specs=[edge_block(wide)] * 3
        + [inv_block(wide), whole((4, 8, width))]
        + [unread()] * 4,
        out_shape=[
            edge_shape,
            edge_shape,
            edge_shape,
            inv_shape,
            vec_shape,
            node_shape,
            node_sums_shape,
            node_shape,
            jax.ShapeDtypeStruct((3 * width, width), BF16),
        ],
        scratch_shapes=[
            pltpu.VMEM((wide, remote), BF16),
            pltpu.VMEM((here, wide), BF16),
            pltpu.VMEM((samples, remote, width), BF16),
            pltpu.VMEM((wide, 128), F32),
            pltpu.VMEM((here, 128), F32),
            pltpu.VMEM((samples, here, width), F32),
            pltpu.VMEM((samples * here, 2 * width), BF16),
            pltpu.VMEM((samples * here, width), BF16),
            pltpu.VMEM((samples * here, width), BF16),
            pltpu.VMEM((samples * here, width), BF16),
            pltpu.VMEM((samples * far, width), F32),
            pltpu.VMEM((far, width), F32),
            pltpu.VMEM((samples, here, width), BF16),
            pltpu.VMEM((samples, here, width), BF16),
            pltpu.VMEM((2 * width, width), BF16),
            pltpu.VMEM((width, width), BF16),
            pltpu.VMEM((samples, here, width), BF16),
            pltpu.VMEM((samples, here, width), F32),
            pltpu.VMEM((samples, here, width), BF16),
            pltpu.VMEM((3 * width, width), BF16),
            pltpu.SemaphoreType.DMA((4,)),
            pltpu.SemaphoreType.DMA((3 * samples + 1,)),
        ],
        compiler_params=params(2),
        cost_estimate=pl.CostEstimate(
            flops=4 * unit, bytes_accessed=8 * samples * edges * width, transcendentals=0
        ),
        name="edge_forward",
    )(
        tiled(wide), node_mask[None], partial, arrived, edge_first, edge_second, vec,
        node_latents, node_cot, node_first, node_second,
    )
    node_parts = scatter_all(node_weights)

    short = edges // 5
    pairs = samples // 2

    def paired(lanes_here):
        return pl.BlockSpec((2, short, lanes_here), lambda i: (i % pairs, i // pairs, 0))

    def early_half(i):
        return (2 * (i % pairs), i // pairs, 0)

    def late_half(i):
        j = jnp.maximum(i - 1, 0)
        return (2 * (j % pairs) + 1, j // pairs, 0)

    (
        hidden_grad, edge_sums, local, remote_sums, received, outbound, edge_weights
    ) = pl.pallas_call(
        edge_backward,
        grid=(edges // short * pairs,),
        in_specs=[
            pl.BlockSpec((1, 8, short), lambda i: (i // pairs, 0, 0)),
            pl.BlockSpec((1, short, width), early_half),
            pl.BlockSpec((1, short, width), late_half),
            paired(width),
            pl.BlockSpec((1, short, width), early_half),
            pl.BlockSpec((1, short, width), late_half),
            paired(width),
            paired(width),
            paired(128),
            pl.BlockSpec((2, here, width), lambda i: (i % pairs, 0, 0)),
            whole((width, width)),
            whole((8, width)),
        ]
        + [unread()] * 3,
        out_specs=[paired(width), whole((4, 8, width))] + [unread()] * 5,
        out_shape=[
            edge_shape,
            vec_shape,
            node_shape,
            jax.ShapeDtypeStruct((samples * far, width), BF16),
            node_shape,
            jax.ShapeDtypeStruct((near, samples * slots, width), BF16),
            jax.ShapeDtypeStruct((4 * width, width), BF16),
        ],
        scratch_shapes=[
            pltpu.VMEM((short, here), BF16),
            pltpu.VMEM((short, min(256, here)), BF16),
            pltpu.VMEM((senders + here, short), BF16),
            pltpu.VMEM((senders + here, short), BF16),
            pltpu.VMEM((width + BLOCK, short), BF16),
            pltpu.VMEM((short, width), BF16),
            pltpu.VMEM((short, width), BF16),
            pltpu.VMEM((short, width), BF16),
            pltpu.VMEM((short, width), BF16),
            pltpu.VMEM((BLOCK, short), BF16),
            pltpu.SMEM((3,), jnp.int32),
            pltpu.VMEM((width, width), BF16),
            pltpu.VMEM((samples, senders + here, width), F32),
            pltpu.VMEM((width, width), F32),
            pltpu.VMEM((width + BLOCK, width), F32),
            pltpu.VMEM((samples * far, width), F32),
            pltpu.VMEM((short, width), BF16),
            pltpu.VMEM((short, width), BF16),
            pltpu.VMEM((width, width), BF16),
            pltpu.VMEM((samples, here, width), BF16),
            pltpu.VMEM((samples * far, width), BF16),
            pltpu.VMEM((samples, here, width), BF16),
            pltpu.VMEM((near, samples * slots, width), BF16),
            pltpu.VMEM((4 * width, width), BF16),
            pltpu.SemaphoreType.DMA((3,)),
            pltpu.SemaphoreType.DMA((6,)),
        ],
        compiler_params=params(1),
        cost_estimate=pl.CostEstimate(
            flops=7 * unit, bytes_accessed=10 * samples * edges * width, transcendentals=0
        ),
        name="edge_backward",
    )(
        tiled(short), edge_latents, edge_latents, edge_cot, act, act, bend, nrm, inv,
        gathered_grad, edge_second, vec,
        edge_latents, act, edge_first,
    )
    node_parts, edge_weights, outbound = lax.optimization_barrier(
        (node_parts, edge_weights, outbound)
    )
    returned = exchange(outbound, -1)
    node_partial, edge_weights = pl.pallas_call(
        edge_totals,
        in_specs=[
            whole((samples, here, width)),
            whole((samples, here, width)),
            whole((samples * far, width)),
            whole((samples, here, width)),
            whole((near, samples * slots, width)),
            whole((samples, here, width)),
            whole((3 * width, width)),
            unread(),
            unread(),
        ],
        out_specs=[whole((samples, here, width)), unread()],
        out_shape=[node_sums_shape, jax.ShapeDtypeStruct((4 * width, width), BF16)],
        input_output_aliases={7: 1},
        scratch_shapes=[pltpu.VMEM((2 * width, width), BF16), pltpu.SemaphoreType.DMA],
        compiler_params=pltpu.CompilerParams(vmem_limit_bytes=VMEM),
        name="edge_totals",
    )(
        local, received, remote_sums, node_latents, arrived, base, edge_first, edge_weights,
        outbound,
    )
    vectors = jnp.concatenate([edge_sums, node_sums]).sum(axis=1)
    count = vectors.shape[0]
    pieces = pair_pieces(edge_weights, vectors)
    node_piece = add_parts(node_parts).astype(BF16)
    pieces, returned, node_piece = lax.optimization_barrier((pieces, returned, node_piece))
    arrived_pieces = exchange_in_side(pieces)
    edge_grad = pl.pallas_call(
        edge_gradient,
        grid=(edges // wide, samples),
        in_specs=[*two_halves(wide), *two_halves(wide), third(0), unread()],
        out_specs=edge_block(wide),
        out_shape=edge_shape,
        scratch_shapes=[pltpu.VMEM((width, width), BF16)],
        compiler_params=params(2),
        cost_estimate=pl.CostEstimate(
            flops=unit, bytes_accessed=6 * samples * edges * width, transcendentals=0
        ),
        name="edge_gradient",
    )(edge_cot, edge_cot, hidden_grad, hidden_grad, edge_first, pieces)
    arrived_pieces, edge_grad = lax.optimization_barrier((arrived_pieces, edge_grad))
    partial_sums = add_parts(arrived_pieces)
    piece = partial_sums.shape[0] - 2 * count
    vectors = split_rows(partial_sums[piece : piece + count] + partial_sums[piece + count :])
    partial_sums = jnp.concatenate([rounded(partial_sums[:piece]), vectors])
    other = swap_sides(jnp.concatenate([partial_sums.astype(BF16), node_piece]))
    totals = partial_sums + other[: piece + 2 * count].astype(F32)
    node_pair = both_sides(node_piece, other[piece + 2 * count :])
    vectors = totals[piece : piece + count] + totals[piece + count :]
    joined = jnp.concatenate([totals[:piece].astype(BF16), node_pair])
    gathered_rows = exchange_in_side(repeat(joined, lax.axis_size("graph") // 2))
    edges_out = pl.pallas_call(
        edge_outputs,
        grid=(edges // wide, samples),
        in_specs=[
            idx_block(wide),
            *two_halves(wide),
            *two_halves(wide),
            whole((8, width)),
            unread(),
        ],
        out_specs=edge_block(wide),
        out_shape=edge_shape,
        scratch_shapes=[pltpu.VMEM((wide, 128), F32)],
        compiler_params=params(2),
        cost_estimate=pl.CostEstimate(
            flops=0, bytes_accessed=6 * samples * edges * width, transcendentals=0
        ),
        name="edge_outputs",
    )(
        tiled(wide), edge_latents, edge_latents, nrm, nrm, vec, joined,
    )
    gathered_rows, edges_out = lax.optimization_barrier((gathered_rows, edges_out))
    nodes_rows = gathered_rows[:, piece:]
    nodes_rows = nodes_rows.reshape(nodes_rows.shape[0], 2, -1, width).transpose(1, 0, 2, 3)
    halves = [
        gathered_rows[:, :piece].reshape(2 * width, width),
        nodes_rows.reshape(-1, width),
    ]
    totals = gather_cores(jnp.concatenate(halves + [split_rows(vectors).astype(BF16)]))
    chunk = width // 2
    parts = 7 * width // chunk
    weights = pl.pallas_call(
        unpack,
        in_specs=[unread()],
        out_specs=[unread()] * 4,
        out_shape=[
            jax.ShapeDtypeStruct((rows * width, width), F32) for rows in (3, 1, 2, 1)
        ],
        scratch_shapes=[
            pltpu.VMEM((parts, chunk, width), BF16),
            pltpu.VMEM((parts, chunk, width), F32),
            pltpu.SemaphoreType.DMA((parts,)),
            pltpu.SemaphoreType.DMA((parts,)),
        ],
        compiler_params=pltpu.CompilerParams(vmem_limit_bytes=VMEM),
        name="unpack",
    )(totals)
    vectors = totals[:, -2 * count :].astype(F32).sum(axis=0)
    vectors = vectors[:count] + vectors[count:]

    node_grad = node_partial + dot_rows(pick, returned.reshape(-1, width)).reshape(
        samples, here, width
    )
    return (
        nodes_out,
        edges_out,
        node_grad,
        edge_grad,
        weights[0],
        vectors[0],
        weights[1],
        vectors[1],
        vectors[2],
        vectors[3],
        weights[2],
        vectors[4],
        weights[3],
        vectors[5],
        vectors[6],
        vectors[7],
    )


def solution(mesh):
    rows = P("dp", "graph", None)
    placed = (rows, rows) + (P(),) * 12 + (rows, rows)
    placed += (P("graph", None, None), P("graph"), P("graph"), P("graph"))
    return jax.shard_map(
        shards,
        mesh=mesh,
        in_specs=placed,
        out_specs=(rows,) * 4 + (P(),) * 12,
        check_vma=False,
    )
```
